32 devices in a mesh: lon: 8 (over y, x, core), lat: 4 (over z).
Axes of the slice: x: 2, y: 2, z: 4, core: 2. Of those that a mesh axis runs over, the one named last changes fastest.
Arguments:
- members: bfloat16 [3, 128, 1440, 128], P(None, 'lat', 'lon'), may hold values from -6 to 6
- background: bfloat16 [3, 128, 1440], P(None, 'lat', 'lon'), may hold values from -6 to 6
Outputs:
- modes: float32 [3, 128, 1440, 128], P(None, 'lat', 'lon')
- r_factor: float32 [128, 128], replicated
The draws below stay inside these ranges and needn't reach their ends.
All inputs are finite; a program needn't handle non-finite values.
Results may differ from the reference program's by a relative error of at most 0.0076.
The reference program's roundings to bfloat16 on the way (of `anomaly`) count: a program that leaves them out, or rounds other values in their place, can miss the bound.
Values may be sent and summed in bfloat16 or wider, within the bound.
No kernel may reach another device: no remote copies, remote signals or barrier semaphores. Data moves between devices by JAX's collectives and lax.ppermute only.
A program may use at most 64 MiB of HBM per device.

```python
import math
import jax
import jax.numpy as jnp
from jax import lax

MEMBERS = 128
FIELDS = 3
LAT = 128
LON = 1440


def shard_levels(key, dims, shards, smallest, top_value):
    loudness = 1.0
    for axis_at, blocks in shards:
        draws = jax.random.uniform(jax.random.fold_in(jax.random.fold_in(key, 6), axis_at), (blocks,), jnp.float32, smallest / len(shards), top_value / len(shards))
        loudness = loudness * jnp.repeat(jnp.exp(draws), dims[axis_at] // blocks).reshape((-1,) + (1,) * (len(dims) - 1 - axis_at))
    return loudness


def centred(stream_key, shape, spread, bound, shards=(), held_as=jnp.bfloat16):
    gain = shard_levels(stream_key, shape, shards, -0.22, 0.18) if shards else 1.0
    entries = jax.random.normal(stream_key, shape, jnp.float32) * spread * gain
    return jnp.minimum(jnp.maximum(entries, -bound), bound).astype(held_as)


def setup_inputs(seed: int = 0) -> dict:
    keys = jax.random.split(jax.random.key(seed), 3)
    members = centred(keys[0], (FIELDS, LAT, LON, MEMBERS), 1.0, 6.0, ((1, 4), (2, 8)))
    background = centred(keys[1], (FIELDS, LAT, LON), 1.0, 6.0, ((1, 4), (2, 8)))
    return {"members": members, "background": background}


def row_coefs(glob, nlat):
    phi = (0.125 * (glob.astype(jnp.float32) + 0.5) - 0.0625 * nlat) * (math.pi / 180.0)
    kx = 0.05 + 0.2 * (1.0 - jnp.cos(phi))
    weight = jnp.sqrt(jnp.cos(phi))
    return (kx.astype(jnp.float32), weight.astype(jnp.float32))

def one_pass(field, kx):
    padded = jnp.pad(field, ((1, 1), (0, 0), (0, 0)))
    padded = jnp.concatenate([padded[:, -1:], padded, padded[:, :1]], axis=1)
    centre = padded[1:-1, 1:-1]
    east_west = padded[1:-1, 2:] + padded[1:-1, :-2] - 2.0 * centre
    north_south = padded[2:, 1:-1] + padded[:-2, 1:-1] - 2.0 * centre
    return centre + kx[:, None, None] * east_west + 0.2 * north_south

def chol_upper(gram):
    order = gram.shape[0]
    index = jnp.arange(order)

    def column(j, lower):
        row_j = lax.dynamic_slice_in_dim(lower, j, 1, 0)[0]
        col_g = lax.dynamic_slice_in_dim(gram, j, 1, 1)[:, 0]
        resid = col_g - jnp.dot(lower, row_j, precision=lax.Precision.HIGHEST)
        pivot = jnp.sqrt(jnp.sum(jnp.where(index == j, resid, 0.0)))
        col_new = jnp.where(index >= j, resid / pivot, 0.0)
        return lower + col_new[:, None] * (index[None, :] == j).astype(jnp.float32)
    lower = lax.fori_loop(0, order, column, jnp.zeros((order, order), jnp.float32))
    return lower.T

def upper_inverse(upper):
    order = upper.shape[0]
    index = jnp.arange(order)
    ident = jnp.eye(order, dtype=jnp.float32)

    def row_step(step, solved):
        i = order - 1 - step
        row_u = lax.dynamic_slice_in_dim(upper, i, 1, 0)[0]
        diag = jnp.sum(jnp.where(index == i, row_u, 0.0))
        above = jnp.where(index > i, row_u, 0.0)
        unit = lax.dynamic_slice_in_dim(ident, i, 1, 0)[0]
        new_row = (unit - jnp.dot(above, solved, precision=lax.Precision.HIGHEST)) / diag
        return solved + (index == i).astype(jnp.float32)[:, None] * new_row[None, :]
    return lax.fori_loop(0, order, row_step, jnp.zeros((order, order), jnp.float32))

def reference(members, background):
    kx, weight = row_coefs(jnp.arange(LAT), LAT)

    def per_field(pair):
        field, ground = pair
        smooth = one_pass(one_pass(field.astype(jnp.float32), kx), kx)
        return ((smooth - ground.astype(jnp.float32)[:, :, None]) * weight[:, None, None]).astype(jnp.bfloat16)
    anomaly = lax.map(per_field, (members, background))
    matrix = anomaly.reshape(-1, MEMBERS)
    gram = jnp.dot(matrix.T, matrix, preferred_element_type=jnp.float32) / (FIELDS * LAT * LON)
    r_factor = chol_upper(gram)
    inverse = upper_inverse(r_factor)
    modes = jnp.dot(matrix, inverse, precision=lax.Precision.HIGHEST, preferred_element_type=jnp.float32)
    return (modes.reshape(FIELDS, LAT, LON, MEMBERS), r_factor)
```

```python
import functools
import math

import jax
import jax.numpy as jnp
from jax import lax
from jax.experimental import pallas as pl
from jax.experimental.pallas import tpu as pltpu
from jax.sharding import PartitionSpec as P

VMEM_LIMIT = 48 * 1024 * 1024
F32 = jnp.float32
BF16 = jnp.bfloat16


def row_coefs(glob, nlat):
    row = jnp.full((8, 128), glob, jnp.int32).astype(F32)
    phi = (0.125 * (row + 0.5) - 0.0625 * nlat) * (math.pi / 180.0)
    cosine = jnp.cos(phi)
    return 0.05 + 0.2 * (1.0 - cosine), jnp.sqrt(cosine)


def rows_of(tile, count):
    return jnp.concatenate([tile] * (count // 8), axis=0)


def stencil_kernel(first_ref, m_ref, north_ref, south_ref, side_ref, bg_ref, a_ref, g_ref,
                   u_ref, v_ref, b_ref, *, nlat):
    rows, cols = m_ref.shape[1], m_ref.shape[2]
    ring = u_ref.shape[1] - 16
    first = first_ref[0]

    def fill(r, value):
        u_ref[r, 8:8 + cols] = value.astype(F32)
        u_ref[r, 8 + cols:12 + cols] = side_ref[0, r]
        u_ref[r, 7:8] = side_ref[0, r, 3:4]
        u_ref[r, 8 + ring:9 + ring] = value[0:1].astype(F32)

    for r in range(2):
        fill(r, north_ref[0, r])
        fill(rows + 2 + r, south_ref[0, r])

    @pl.loop(0, rows)
    def _(j):
        fill(j + 2, m_ref[0, j])

    @pl.loop(1, rows + 3)
    def _(r):
        glob = first + r - 2
        kx, _ = row_coefs(glob, nlat)
        inside = jnp.full((8, 128), (glob >= 0) & (glob < nlat), jnp.bool_)
        c = rows_of(jnp.where(inside, 3.0 - 10.0 * kx, 0.0), ring)
        k = rows_of(jnp.where(inside, 5.0 * kx, 0.0), ring)
        one = rows_of(jnp.where(inside, 1.0, 0.0), ring)
        v = (one * (u_ref[r - 1, 8:8 + ring] + u_ref[r + 1, 8:8 + ring]) + c * u_ref[r, 8:8 + ring]
             + k * (u_ref[r, 7:7 + ring] + u_ref[r, 9:9 + ring]))
        v_ref[r, 8:8 + ring] = v
        v_ref[r, 7:8] = v[ring - 1:ring]
        v_ref[r, 8 + ring:9 + ring] = v[0:1]

    live = lax.broadcasted_iota(jnp.int32, (ring, 128), 0) < cols
    pick = lax.broadcasted_iota(jnp.int32, (rows, 128), 0)

    @pl.loop(0, rows)
    def _(j):
        r = j + 2
        kx, weight = row_coefs(first + j, nlat)
        c = rows_of(3.0 - 10.0 * kx, ring)
        k = rows_of(5.0 * kx, ring)
        w = rows_of(weight, ring)
        ground = lax.dot_general(bg_ref[0], (pick == j).astype(BF16), (((0,), (0,)), ((), ())),
                                 preferred_element_type=F32)
        y = (v_ref[r - 1, 8:8 + ring] + v_ref[r + 1, 8:8 + ring] + c * v_ref[r, 8:8 + ring]
             + k * (v_ref[r, 7:7 + ring] + v_ref[r, 9:9 + ring]))
        a = jnp.where(live, (y * 0.04 - ground) * w, 0.0)
        b_ref[j, 0:ring] = a
        b_ref[j, ring:] = jnp.zeros((b_ref.shape[1] - ring, 128), F32)
        a_ref[j] = b_ref[j].astype(BF16)

    flat = a_ref[...].reshape(-1, 128)
    gram = lax.dot_general(flat, flat, (((0,), (0,)), ((), ())), preferred_element_type=F32)

    @pl.when(pl.program_id(0) == 0)
    def _():
        g_ref[...] = gram

    @pl.when(pl.program_id(0) > 0)
    def _():
        g_ref[...] += gram


def factor(g):
    n = 128
    lane = lax.broadcasted_iota(jnp.int32, (8, n), 1)
    sub = lax.broadcasted_iota(jnp.int32, (8, n), 0)
    w = list(g)
    tiles = len(w)
    for b0 in range(tiles):
        cols = [[jnp.broadcast_to(w[b][:, 8 * b0 + j:8 * b0 + j + 1], (8, n)) for b in range(b0, tiles)]
                for j in range(8)]
        for s in range(8):
            k = 8 * b0 + s
            inverse = 1.0 / jnp.broadcast_to(cols[s][0][s:s + 1], (8, n))
            pivot_row = jnp.where(lane == k, 1.0, jnp.broadcast_to(w[b0][s:s + 1], (8, n)))
            rows = [jnp.broadcast_to(cols[j][0][s:s + 1], (8, n)) for j in range(s + 1, 8)]
            for b in range(b0, tiles):
                i = b - b0
                f = cols[s][i] * inverse
                if i == 0:
                    if s == 7:
                        continue
                    f = jnp.where(sub > s, f, 0.0)
                    kept = jnp.where((lane == k) & (sub > s), 0.0, w[b])
                else:
                    kept = jnp.where(lane == k, 0.0, w[b])
                w[b] = kept - f * pivot_row
                for j in range(s + 1, 8):
                    cols[j][i] = cols[j][i] - f * rows[j - s - 1]
    r, x = [], []
    for b in range(tiles):
        diag = lane == sub + 8 * b
        scale = lax.rsqrt(jnp.sum(jnp.where(diag, w[b], 0.0), axis=1, keepdims=True))
        r.append(jnp.where(lane >= sub + 8 * b, w[b] * scale, 0.0))
        x.append(jnp.where(diag, scale, jnp.where(lane < sub + 8 * b, w[b] * scale, 0.0)))
    return jnp.concatenate(r, axis=0), jnp.concatenate(x, axis=0)


def modes_kernel(core_ref, own_ref, other_ref, a_hbm, out_ref, r_ref, a_ref, x_ref, sem, *, total):
    step = pl.program_id(0)
    lats, cols = out_ref.shape[1], out_ref.shape[2]
    copy = pltpu.make_async_copy(a_hbm, a_ref, sem)

    @pl.when(step == 0)
    def _():
        copy.start()
        own = jnp.full((8, 128), core_ref[0], jnp.int32) == 1
        g = [jnp.where(own, own_ref[8 * b:8 * b + 8], other_ref[8 * b:8 * b + 8]) * (1.0 / total)
             for b in range(16)]
        r, x = factor(g)
        r_ref[...] = r
        inv = x.T
        high = inv.astype(BF16)
        x_ref[0] = high
        x_ref[1] = (inv - high.astype(F32)).astype(BF16)
        copy.wait()

    a = a_ref[pl.ds(step * lats, lats)].reshape(-1, 128)
    m = jnp.dot(a, x_ref[0], preferred_element_type=F32) + jnp.dot(a, x_ref[1], preferred_element_type=F32)
    out_ref[0] = m.reshape(lats, -1, 128)[:, :cols]


def halos(members):
    lat, lon = lax.axis_size("lat"), lax.axis_size("lon")
    north = [(i, i + 1) for i in range(lat - 1)]
    south = [(i + 1, i) for i in range(lat - 1)]
    east = [((i + 1) % lon, i) for i in range(lon)]
    west = [(i, (i + 1) % lon) for i in range(lon)]
    from_north = lax.ppermute(members[:, -2:], "lat", north)
    from_south = lax.ppermute(members[:, :2], "lat", south)
    from_east = lax.ppermute(members[:, :, :2], "lon", east)
    from_west = lax.ppermute(members[:, :, -2:], "lon", west)
    ends = jnp.concatenate([from_north, from_south], axis=1)
    ends_east = lax.ppermute(ends[:, :, :2], "lon", east)
    ends_west = lax.ppermute(ends[:, :, -2:], "lon", west)
    side = jnp.concatenate([from_east, from_west], axis=2)
    corner = jnp.concatenate([ends_east, ends_west], axis=2)
    side = jnp.concatenate([corner[:, :2], side, corner[:, 2:]], axis=1)
    return from_north, from_south, side.astype(F32)


def total_gram(gram):
    lat, lon = lax.axis_size("lat"), lax.axis_size("lon")
    gram = gram + lax.ppermute(gram, "lon", [(i, i + 1) for i in range(0, lon, 2)])
    step = 2
    while step < lon:
        gram = gram + lax.ppermute(gram, "lon", [(i, i ^ step) for i in range(1, lon, 2)])
        step *= 2
    step = 1
    while step < lat:
        pairs = [(k * lat + i, k * lat + (i ^ step)) for k in range(1, lon, 2) for i in range(lat)]
        gram = gram + lax.ppermute(gram, ("lon", "lat"), pairs)
        step *= 2
    other = lax.ppermute(gram, "lon", [(i + 1, i) for i in range(0, lon, 2)])
    return gram, other


def local(members, background):
    fields, rows, cols, width = members.shape
    lat, lon = lax.axis_size("lat"), lax.axis_size("lon")
    nlat = rows * lat
    ring = -(-(cols + 4) // 8) * 8
    held = -(-ring // 16) * 16
    first = (lax.axis_index("lat") * rows).astype(jnp.int32).reshape(1)
    north, south, side = halos(members)
    ground = jnp.pad(background, ((0, 0), (0, 0), (0, ring - cols)))
    vmem = functools.partial(pltpu.VMEM)
    a, gram = pl.pallas_call(
        functools.partial(stencil_kernel, nlat=nlat),
        grid=(fields,),
        out_shape=(jax.ShapeDtypeStruct((fields * rows, held, width), BF16),
                   jax.ShapeDtypeStruct((width, width), F32)),
        in_specs=[
            pl.BlockSpec(memory_space=pltpu.SMEM),
            pl.BlockSpec((1, rows, cols, width), lambda f: (f, 0, 0, 0)),
            pl.BlockSpec((1, 2, cols, width), lambda f: (f, 0, 0, 0)),
            pl.BlockSpec((1, 2, cols, width), lambda f: (f, 0, 0, 0)),
            pl.BlockSpec((1, rows + 4, 4, width), lambda f: (f, 0, 0, 0)),
            pl.BlockSpec((1, rows, ring), lambda f: (f, 0, 0)),
        ],
        out_specs=(pl.BlockSpec((rows, held, width), lambda f: (f, 0, 0)),
                   pl.BlockSpec((width, width), lambda f: (0, 0))),
        scratch_shapes=[vmem((rows + 4, ring + 16, width), F32), vmem((rows + 4, ring + 16, width), F32),
                        vmem((rows, held, width), F32)],
        compiler_params=pltpu.CompilerParams(vmem_limit_bytes=VMEM_LIMIT),
    )(first, members, north, south, side, ground)
    own, other = total_gram(gram)
    core = (lax.axis_index("lon") % 2).astype(jnp.int32).reshape(1)
    lats = 8
    per = rows // lats
    modes, r_factor = pl.pallas_call(
        functools.partial(modes_kernel, total=float(fields * nlat * cols * lon)),
        grid=(fields * per,),
        out_shape=(jax.ShapeDtypeStruct(members.shape, F32), jax.ShapeDtypeStruct((width, width), F32)),
        in_specs=[
            pl.BlockSpec(memory_space=pltpu.SMEM),
            pl.BlockSpec((width, width), lambda s: (0, 0)),
            pl.BlockSpec((width, width), lambda s: (0, 0)),
            pl.BlockSpec(memory_space=pl.ANY),
        ],
        out_specs=(pl.BlockSpec((1, lats, cols, width), lambda s: (s // per, s % per, 0, 0)),
                   pl.BlockSpec((width, width), lambda s: (0, 0))),
        scratch_shapes=[vmem((fields * rows, held, width), BF16), vmem((2, width, width), BF16),
                        pltpu.SemaphoreType.DMA],
        compiler_params=pltpu.CompilerParams(vmem_limit_bytes=VMEM_LIMIT),
    )(core, own, other, a)
    return modes, r_factor


def solution(mesh):
    return jax.shard_map(
        local,
        mesh=mesh,
        in_specs=(P(None, "lat", "lon", None), P(None, "lat", "lon")),
        out_specs=(P(None, "lat", "lon", None), P()),
        check_vma=False,
    )
```

```python
import functools
import math

import jax
import jax.numpy as jnp
from jax import lax
from jax.experimental import pallas as pl
from jax.experimental.pallas import tpu as pltpu
from jax.sharding import PartitionSpec as P

VMEM_LIMIT = 40 * 1024 * 1024
F32 = jnp.float32
BF16 = jnp.bfloat16
TILE = (8, 128)


def row_coefs(glob, nlat):
    phi = (0.125 * (glob.astype(F32) + 0.5) - 0.0625 * nlat) * (math.pi / 180.0)
    cosine = jnp.cos(phi)
    return 0.05 + 0.2 * (1.0 - cosine), jnp.sqrt(cosine)


def scaled_coefs(glob, nlat):
    kx, weight = row_coefs(glob, nlat)
    return 3.0 - 10.0 * kx, 5.0 * kx, weight


def sublane():
    return lax.broadcasted_iota(jnp.int32, TILE, 0)


def tiles_of(x):
    return [x[8 * t:8 * t + 8] for t in range(x.shape[0] // 8)]


def neighbours(x, above, below):
    sub = sublane()
    down = [pltpu.roll(t, 1, 0) for t in x]
    up = [pltpu.roll(t, 7, 0) for t in x]
    out = []
    for i in range(len(x)):
        north = jnp.where(sub == 0, down[i - 1] if i else above, down[i])
        south = jnp.where(sub == 7, up[i + 1] if i + 1 < len(x) else below, up[i])
        out.append(north + south)
    return out


def gram_of(a):
    return lax.dot_general(a, a, (((0,), (0,)), ((), ())), preferred_element_type=F32)


def inner_kernel(first_ref, m_ref, bg_ref, a_ref, en_ref, es_ref, g_ref, coef_ref, bgf_ref, *, nlat, group):
    cols, rows = m_ref.shape[1], m_ref.shape[2]
    nt = rows // 8
    first = first_ref[0]
    sub = sublane()
    for t in range(nt):
        c, k, w = scaled_coefs(first + 8 * t + sub, nlat)
        live = (8 * t + sub >= 2) & (8 * t + sub < rows - 2)
        coef_ref[0, t], coef_ref[1, t] = c, k
        coef_ref[2, t], coef_ref[3, t] = 0.04 * w, w
        coef_ref[4, t], coef_ref[5, t] = jnp.where(live, 0.04 * w, 0.0), jnp.where(live, w, 0.0)
    bgf_ref[:, 0:cols] = bg_ref[0].astype(F32)
    north_in = jnp.where(jnp.full(TILE, first, jnp.int32) > 0, 1.0, 0.0)
    south_in = jnp.where(jnp.full(TILE, first, jnp.int32) + rows < nlat, 1.0, 0.0)
    zero = jnp.zeros(TILE, F32)
    width = bgf_ref.shape[1]

    def load(l):
        return tiles_of(m_ref[0, l].astype(F32))

    def body(g, carry):
        u0, u1, v0, v1, gram = carry
        base = g * group
        ground = pltpu.roll(bgf_ref[...], lax.rem(width + 1 - base, width), 1)
        made = []
        for i in range(group):
            u2 = load(jnp.minimum(base + i + 1, cols - 1))
            ns = neighbours(u1, zero, zero)
            v2 = [ns[t] + coef_ref[0, t] * u1[t] + coef_ref[1, t] * (u0[t] + u2[t]) for t in range(nt)]
            ns = neighbours(v1, north_in * pltpu.roll(u0[0], 0, 0), south_in * u0[nt - 1])
            y = [ns[t] + coef_ref[0, t] * v1[t] + coef_ref[1, t] * (v0[t] + v2[t]) for t in range(nt)]
            b = [jnp.broadcast_to(ground[8 * t:8 * t + 8, i:i + 1], TILE) for t in range(nt)]
            a = jnp.concatenate([y[t] * coef_ref[4, t] - b[t] * coef_ref[5, t] for t in range(nt)],
                                axis=0).astype(BF16)
            a_ref[0, jnp.maximum(base + i - 1, 0)] = a
            e = y[0] * coef_ref[2, 0] - b[0] * coef_ref[3, 0]
            en_ref.at[0, pl.ds(pl.multiple_of(g * 2 * group, 8), 2 * group)][2 * i:2 * i + 2] = e[0:2]
            e = y[nt - 1] * coef_ref[2, nt - 1] - b[nt - 1] * coef_ref[3, nt - 1]
            es_ref.at[0, pl.ds(pl.multiple_of(g * 2 * group, 8), 2 * group)][2 * i:2 * i + 2] = e[6:8]
            made.append(a)
            u0, u1, v0, v1 = u1, u2, v1, v2
        if True:
            for i in (0, 1, 2):
                made[i] = jnp.where(jnp.full((rows, 128), base + i - 1, jnp.int32) >= 2, made[i], jnp.zeros_like(made[i]))
            i = group - 1
            made[i] = jnp.where(jnp.full((rows, 128), base + i - 1, jnp.int32) < cols - 2, made[i],
                                jnp.zeros_like(made[i]))
        gram = gram + gram_of(jnp.concatenate(made, axis=0))
        return u0, u1, v0, v1, gram

    u = load(0)
    start = ([zero] * nt, u, [zero] * nt, [zero] * nt, jnp.zeros((128, 128), F32))
    gram = lax.fori_loop(0, cols // group, body, start)[4]
    for l in (0, 1, cols - 2, cols - 1):
        a_ref[0, l] = jnp.zeros((rows, 128), BF16)

    @pl.when(pl.program_id(0) == 0)
    def _():
        g_ref[...] = gram

    @pl.when(pl.program_id(0) > 0)
    def _():
        g_ref[...] += gram


def pack(g):
    lane = lax.broadcasted_iota(jnp.int32, (32, 128), 1)
    middle = jnp.where(lane < 32, pltpu.roll(g[96:128], 32, 1), g[32:64])
    last = jnp.where(lane[:16] < 64, pltpu.roll(g[80:96], 64, 1), g[64:80])
    return jnp.concatenate([g[0:32], middle, last], axis=0)


def unpack(p):
    upper = jnp.concatenate([p[0:80], pltpu.roll(p[64:80], 64, 1), pltpu.roll(p[32:64], 96, 1)], axis=0)
    row = lax.broadcasted_iota(jnp.int32, (128, 128), 0)
    col = lax.broadcasted_iota(jnp.int32, (128, 128), 1)
    return jnp.where(col >= row, upper, upper.T)


def outer_kernel(first_ref, en_ref, es_ref, n_ref, s_ref, x_ref, bg_ref, gin_ref, an_ref, as_ref, ac_ref, g_ref,
                 pad_ref, *, nlat):
    fields, pairs = n_ref.shape[0], n_ref.shape[1]
    rows, cols = bg_ref.shape[1], bg_ref.shape[2]
    first = first_ref[0]
    nt = rows // 8
    sub = sublane()
    gram = gin_ref[...]
    where = lax.broadcasted_iota(jnp.int32, (pairs, 128), 0)
    inside = (where >= 4) & (where < pairs - 4)

    def splat(row):
        return jnp.full((8, 128), row, jnp.int32)

    for e_ref, h_ref, out_ref, near, halo, par, sign in ((en_ref, n_ref, an_ref, 0, -1, 0, 1),
                                                         (es_ref, s_ref, as_ref, rows - 1, rows, 1, -1)):
        c0, k0, _ = scaled_coefs(splat(first + near), nlat)
        c1, k1, _ = scaled_coefs(splat(first + halo), nlat)
        _, _, wa = scaled_coefs(splat(first + near) + (sub % 2 - par), nlat)
        many = pairs // 8
        c = jnp.concatenate([c0 + c1] * many, axis=0)
        k = jnp.concatenate([k0 + k1] * many, axis=0)
        w = jnp.concatenate([0.04 * wa] * many, axis=0)
        outermost = where % 2 == par
        for f in range(fields):
            h = h_ref[f].astype(F32)
            pad_ref[8:8 + pairs] = h
            nearer = pad_ref[8 + sign:8 + sign + pairs]
            wide = pad_ref[8 + sign - 2:8 + sign - 2 + pairs] + pad_ref[8 + sign + 2:8 + sign + 2 + pairs]
            more = h + jnp.where(outermost, c * nearer + k * wide, 0.0)
            made = jnp.where(inside, e_ref[f, 2:2 + pairs] + w * more, 0.0).astype(BF16)
            out_ref[f] = made
            gram = gram + gram_of(made)

    coefs = [scaled_coefs(first + 8 * t + sub, nlat) for t in range(nt)]
    beyond = first + rows + jnp.where(sub < 4, sub, sub - 8 - rows)
    c, k, _ = scaled_coefs(beyond, nlat)
    real = (beyond >= 0) & (beyond < nlat)
    vc = [x[0] for x in coefs] + [jnp.where(real, c, 0.0)]
    vk = [x[1] for x in coefs] + [jnp.where(real, k, 0.0)]
    one = jnp.where(real, 1.0, 0.0)
    for f in range(fields):
        bg = bg_ref[f].astype(F32)
        for side in range(2):
            u = [tiles_of(x_ref[f, 6 * side + l]) for l in range(6)]
            v = []
            for l in range(1, 5):
                ns = neighbours(u[l], pltpu.roll(u[l][nt], 1, 0), pltpu.roll(u[l][0], 7, 0))
                ns[nt] = one * ns[nt]
                v.append([ns[t] + vc[t] * u[l][t] + vk[t] * (u[l - 1][t] + u[l + 1][t]) for t in range(nt + 1)])
            for l in range(2):
                ns = neighbours(v[l + 1], pltpu.roll(v[l + 1][nt], 1, 0), pltpu.roll(v[l + 1][0], 7, 0))
                at = l + side * (cols - 2)
                parts = []
                for t in range(nt):
                    y = ns[t] + vc[t] * v[l + 1][t] + vk[t] * (v[l][t] + v[l + 2][t])
                    b = jnp.broadcast_to(bg[8 * t:8 * t + 8, at:at + 1], TILE)
                    parts.append((0.04 * y - b) * coefs[t][2])
                ac_ref[f, 2 * side + l] = jnp.concatenate(parts, axis=0).astype(BF16)
    gram = gram + gram_of(ac_ref[...].reshape(-1, 128))
    g_ref[...] = pack(gram)


def factor(g):
    n = 128
    lane = lax.broadcasted_iota(jnp.int32, (8, n), 1)
    sub = lax.broadcasted_iota(jnp.int32, (8, n), 0)
    w = list(g)
    tiles = len(w)
    for b0 in range(tiles):
        cols = [[jnp.broadcast_to(w[b][:, 8 * b0 + j:8 * b0 + j + 1], (8, n)) for b in range(b0, tiles)]
                for j in range(8)]
        for s in range(8):
            k = 8 * b0 + s
            inverse = 1.0 / jnp.broadcast_to(cols[s][0][s:s + 1], (8, n))
            pivot_row = jnp.where(lane == k, 1.0, jnp.broadcast_to(w[b0][s:s + 1], (8, n)))
            rows = [jnp.broadcast_to(cols[j][0][s:s + 1], (8, n)) for j in range(s + 1, 8)]
            for b in range(b0, tiles):
                i = b - b0
                f = cols[s][i] * inverse
                if i == 0:
                    if s == 7:
                        continue
                    f = jnp.where(sub > s, f, 0.0)
                    kept = jnp.where((lane == k) & (sub > s), 0.0, w[b])
                else:
                    kept = jnp.where(lane == k, 0.0, w[b])
                w[b] = kept - f * pivot_row
                for j in range(s + 1, 8):
                    cols[j][i] = cols[j][i] - f * rows[j - s - 1]
    r, x = [], []
    for b in range(tiles):
        diag = lane == sub + 8 * b
        scale = lax.rsqrt(jnp.sum(jnp.where(diag, w[b], 0.0), axis=1, keepdims=True))
        r.append(jnp.where(lane >= sub + 8 * b, w[b] * scale, 0.0))
        x.append(jnp.where(diag, scale, jnp.where(lane < sub + 8 * b, w[b] * scale, 0.0)))
    return jnp.concatenate(r, axis=0), jnp.concatenate(x, axis=0)


def modes_kernel(p_ref, an_ref, as_ref, ac_hbm, a_hbm, out_ref, r_ref, a_ref, x_ref, sems, *, total):
    step = pl.program_id(0)
    lons, rows = out_ref.shape[1], out_ref.shape[2]
    fields, cols = a_ref.shape[0], a_ref.shape[1]
    per = cols // lons

    @pl.when(step == 0)
    def _():
        copy = pltpu.make_async_copy(a_hbm, a_ref, sems.at[0])
        copy.start()
        g = unpack(p_ref[...]) * (1.0 / total)
        r, x = factor(tiles_of(g))
        r_ref[...] = r
        inv = x.T
        high = inv.astype(BF16)
        x_ref[0] = high
        x_ref[1] = (inv - high.astype(F32)).astype(BF16)
        copy.wait()
        sides = [pltpu.make_async_copy(ac_hbm.at[:, pl.ds(2 * s, 2)], a_ref.at[:, pl.ds(s * (cols - 2), 2)],
                                       sems.at[1 + s]) for s in range(2)]
        for side in sides:
            side.start()
        for side in sides:
            side.wait()

    def times(a):
        return jnp.dot(a, x_ref[0], preferred_element_type=F32) + jnp.dot(a, x_ref[1], preferred_element_type=F32)

    f, part = lax.div(step, per), lax.rem(step, per)
    a = a_ref[f, pl.ds(part * lons, lons)].reshape(-1, 128)
    out_ref[0] = times(a).reshape(lons, rows, 128)
    north, south = times(an_ref[0]), times(as_ref[0])
    for l in range(lons):
        def put(l=l):
            out_ref[0, l, 0:2] = north[2 * l:2 * l + 2]
            out_ref[0, l, rows - 2:rows] = south[2 * l:2 * l + 2]
        if l < 2:
            pl.when(part > 0)(put)
        elif l >= lons - 2:
            pl.when(part < per - 1)(put)
        else:
            put()


def shifts(count, wrap):
    ahead = [(i, (i + 1) % count) for i in range(count if wrap else count - 1)]
    return ahead, [(j, i) for i, j in ahead]


def halos(m):
    fields, cols, rows, width = m.shape
    down, up = shifts(lax.axis_size("lat"), False)
    east, west = shifts(lax.axis_size("lon"), True)
    north = lax.ppermute(m[:, :, rows - 2:].reshape(fields, 2 * cols, width), "lat", down)
    south = lax.ppermute(m[:, :, :2].reshape(fields, 2 * cols, width), "lat", up)
    from_west = lax.ppermute(m[:, cols - 2:], "lon", east)
    from_east = lax.ppermute(m[:, :2], "lon", west)
    both = jnp.concatenate([from_west, from_east], axis=1)
    corner_north = lax.ppermute(both[:, :, rows - 2:], "lat", down)
    corner_south = lax.ppermute(both[:, :, :2], "lat", up)
    n4 = north.reshape(fields, cols, 2, width)
    s4 = south.reshape(fields, cols, 2, width)
    zero = jnp.zeros((fields, 12, 4, width), BF16)

    def around(sides, whole):
        return jnp.concatenate([sides[:, :2], whole[:, :4], whole[:, cols - 4:], sides[:, 2:]], axis=1)

    ring = jnp.concatenate([around(both, m), around(corner_south, s4), zero, around(corner_north, n4)], axis=2)
    return north, south, ring.astype(F32)


def total_gram(gram):
    for axis in ("lon", "lat"):
        size, step = lax.axis_size(axis), 1
        while step < size:
            gram = gram + lax.ppermute(gram, axis, [(i, i ^ step) for i in range(size)])
            step *= 2
    return gram


def whole(*shape):
    return pl.BlockSpec(shape, lambda *_: (0,) * len(shape))


def local(members, background):
    fields, rows, cols, width = members.shape
    lat, lon = lax.axis_size("lat"), lax.axis_size("lon")
    nlat = rows * lat
    group = 12
    per = 4
    lons = cols // per
    first = (lax.axis_index("lat") * rows).astype(jnp.int32).reshape(1)
    m = jnp.transpose(members, (0, 2, 1, 3))
    north, south, ring = halos(m)
    smem = pl.BlockSpec(memory_space=pltpu.SMEM)
    params = pltpu.CompilerParams(vmem_limit_bytes=VMEM_LIMIT)
    pairs = 2 * cols
    a, en, es, gram = pl.pallas_call(
        functools.partial(inner_kernel, nlat=nlat, group=group),
        grid=(fields,),
        out_shape=(jax.ShapeDtypeStruct((fields, cols, rows, width), BF16),
                   jax.ShapeDtypeStruct((fields, pairs + 8, width), F32),
                   jax.ShapeDtypeStruct((fields, pairs + 8, width), F32),
                   jax.ShapeDtypeStruct((width, width), F32)),
        in_specs=[smem,
                  pl.BlockSpec((1, cols, rows, width), lambda f: (f, 0, 0, 0)),
                  pl.BlockSpec((1, rows, cols), lambda f: (f, 0, 0))],
        out_specs=(pl.BlockSpec((1, cols, rows, width), lambda f: (f, 0, 0, 0)),
                   pl.BlockSpec((1, pairs + 8, width), lambda f: (f, 0, 0)),
                   pl.BlockSpec((1, pairs + 8, width), lambda f: (f, 0, 0)),
                   whole(width, width)),
        scratch_shapes=[pltpu.VMEM((6, rows // 8, 8, 128), F32), pltpu.VMEM((rows, -(-cols // 128) * 128), F32)],
        compiler_params=params,
        cost_estimate=pl.CostEstimate(flops=2 * fields * cols * rows * width * width,
                                      bytes_accessed=5 * fields * cols * rows * width, transcendentals=0),
    )(first, m, background)
    an, as_, ac, packed = pl.pallas_call(
        functools.partial(outer_kernel, nlat=nlat),
        grid=(1,),
        out_shape=(jax.ShapeDtypeStruct((fields, pairs, width), BF16),
                   jax.ShapeDtypeStruct((fields, pairs, width), BF16),
                   jax.ShapeDtypeStruct((fields, 4, rows, width), BF16),
                   jax.ShapeDtypeStruct((80, width), F32)),
        in_specs=[smem, whole(fields, pairs + 8, width), whole(fields, pairs + 8, width),
                  whole(fields, pairs, width), whole(fields, pairs, width),
                  whole(fields, 12, rows + 8, width), whole(fields, rows, cols), whole(width, width)],
        out_specs=(whole(fields, pairs, width), whole(fields, pairs, width),
                   whole(fields, 4, rows, width), whole(80, width)),
        scratch_shapes=[pltpu.VMEM((pairs + 16, width), F32)],
        compiler_params=params,
    )(first, en, es, north, south, ring, background, gram)
    packed = total_gram(packed)
    any_place = pl.BlockSpec(memory_space=pl.ANY)
    split = fields * per
    edge = pl.BlockSpec((1, 2 * lons, width), lambda s: (s, 0, 0))
    modes, r_factor = pl.pallas_call(
        functools.partial(modes_kernel, total=float(fields * nlat * cols * lon)),
        grid=(split,),
        out_shape=(jax.ShapeDtypeStruct((fields, cols, rows, width), F32),
                   jax.ShapeDtypeStruct((width, width), F32)),
        in_specs=[whole(80, width), edge, edge, any_place, any_place],
        out_specs=(pl.BlockSpec((1, lons, rows, width), lambda s: (s // per, s % per, 0, 0)),
                   whole(width, width)),
        scratch_shapes=[pltpu.VMEM((fields, cols, rows, width), BF16), pltpu.VMEM((2, width, width), BF16),
                        pltpu.SemaphoreType.DMA((3,))],
        compiler_params=params,
    )(packed, an.reshape(split, 2 * lons, width), as_.reshape(split, 2 * lons, width), ac, a)
    return jnp.transpose(modes, (0, 2, 1, 3)), r_factor


def solution(mesh):
    return jax.shard_map(
        local,
        mesh=mesh,
        in_specs=(P(None, "lat", "lon", None), P(None, "lat", "lon")),
        out_specs=(P(None, "lat", "lon", None), P()),
        check_vma=False,
    )
```

```python
import functools
import math

import jax
import jax.numpy as jnp
from jax import lax
from jax.experimental import pallas as pl
from jax.experimental.pallas import tpu as pltpu
from jax.sharding import PartitionSpec as P

VMEM_LIMIT = 32 * 1024 * 1024
F32 = jnp.float32
BF16 = jnp.bfloat16
TILE = (8, 128)


def row_coefs(glob, nlat):
    phi = (0.125 * (glob.astype(F32) + 0.5) - 0.0625 * nlat) * (math.pi / 180.0)
    cosine = jnp.cos(phi)
    return 0.05 + 0.2 * (1.0 - cosine), jnp.sqrt(cosine)


def scaled_coefs(glob, nlat):
    kx, weight = row_coefs(glob, nlat)
    return 3.0 - 10.0 * kx, 5.0 * kx, weight


def sublane():
    return lax.broadcasted_iota(jnp.int32, TILE, 0)


def tiles_of(x):
    return [x[8 * t:8 * t + 8] for t in range(x.shape[0] // 8)]


def neighbours(x, above, below):
    sub = sublane()
    down = [pltpu.roll(t, 1, 0) for t in x]
    up = [pltpu.roll(t, 7, 0) for t in x]
    out = []
    for i in range(len(x)):
        north = jnp.where(sub == 0, down[i - 1] if i else above, down[i])
        south = jnp.where(sub == 7, up[i + 1] if i + 1 < len(x) else below, up[i])
        out.append(north + south)
    return out


def gram_of(a):
    return lax.dot_general(a, a, (((0,), (0,)), ((), ())), preferred_element_type=F32)


def fetch_kernel(place_ref, m_hbm, m_ref, lon_a_ref, lon_b_ref, lat_a_ref, lat_b_ref, low_ref, high_ref, sems):
    fields, cols, rows, width = m_ref.shape
    lon_even = lax.rem(place_ref[0], 2) == 0
    lat_even = lax.rem(place_ref[1], 2) == 0
    copies = [pltpu.make_async_copy(m_hbm.at[f], m_ref.at[f], sems.at[f]) for f in range(fields)]
    for copy in copies:
        copy.start()
    for f in range(fields):
        copies[f].wait()
        first, last = m_ref[f, 0:2], m_ref[f, cols - 2:cols]
        lon_a_ref[f] = jnp.where(lon_even, last, first)
        lon_b_ref[f] = jnp.where(lon_even, first, last)
        for l in range(cols):
            low_ref[2 * l:2 * l + 2] = m_ref[f, l, 0:16].astype(F32)[0:2]
            high_ref[2 * l:2 * l + 2] = m_ref[f, l, rows - 16:rows].astype(F32)[14:16]
        low, high = low_ref[...], high_ref[...]
        lat_a_ref[f] = jnp.where(lat_even, high, low).astype(BF16)
        lat_b_ref[f] = jnp.where(lat_even, low, high).astype(BF16)


def inner_kernel(place_ref, m_ref, bg_ref, a_ref, en_ref, es_ref, g_ref, mat_ref, coef_ref, entries_ref, *, nlat):
    cols, rows = m_ref.shape[1], m_ref.shape[2]
    wide = 2
    nt = rows // 8
    first = place_ref[1] * rows

    sub = sublane()
    lane = lax.broadcasted_iota(jnp.int32, TILE, 1)
    for t in range(nt):
        row = 8 * t + sub
        glob = first + row
        c, k, w = scaled_coefs(glob, nlat)
        cn, kn, _ = scaled_coefs(glob - 1, nlat)
        cs, ks, _ = scaled_coefs(glob + 1, nlat)
        live = (row >= 2) & (row < rows - 2)
        coef_ref[0, t], coef_ref[1, t] = 0.04 * w, w
        coef_ref[2, t], coef_ref[3, t] = jnp.where(live, 0.04 * w, 0.0), jnp.where(live, w, 0.0)
        both = jnp.where((glob == 0) | (glob == nlat - 1), 1.0, 2.0)
        dj = lax.rem(lane, rows) - row
        for i in range(4):
            for half in range(2):
                dl = jnp.abs(4 * half + lax.div(lane, rows) - i - 2)
                by_lon = lambda zero, one, two: jnp.where(
                    dl == 0, zero, jnp.where(dl == 1, one, jnp.where(dl == 2, two, 0.0)))
                entry = jnp.where(
                    dj == 0, by_lon(both + c * c + 2.0 * k * k, 2.0 * c * k, k * k), jnp.where(
                        dj == -1, by_lon(c + cn, k + kn, 0.0), jnp.where(
                            dj == 1, by_lon(c + cs, k + ks, 0.0), jnp.where(
                                (jnp.abs(dj) == 2) & (dl == 0), 1.0, 0.0))))
                high = entry.astype(BF16).astype(F32)
                at = pl.ds(rows * i + 8 * t, 8), pl.ds(128 * half, 128)
                entries_ref[at[0], at[1]] = high
                entries_ref[pl.ds(128 + rows * i + 8 * t, 8), at[1]] = entry - high
    mat_ref[...] = entries_ref[...].astype(BF16)

    def field(f, gram):
        ground = bg_ref[f].astype(F32)
        for l in (0, 1, cols - 2, cols - 1):
            a_ref[f, l] = jnp.zeros((rows, 128), BF16)
        for l0 in range(2, cols - 2, 4 * wide):
            chunk = [m_ref[f, l - 2:l + 6].reshape(256, 128) for l in range(l0, min(l0 + 4 * wide, cols - 2), 4)]
            y = jnp.dot(mat_ref[...], jnp.concatenate(chunk, axis=1), preferred_element_type=F32)
            y = y[:128] + y[128:]
            for q in range(len(chunk)):
                made = []
                for i in range(4):
                    l = l0 + 4 * q + i
                    for t in range(nt):
                        yt = y[rows * i + 8 * t:rows * i + 8 * t + 8, 128 * q:128 * q + 128]
                        b = jnp.broadcast_to(ground[8 * t:8 * t + 8, l:l + 1], TILE)
                        made.append(yt * coef_ref[2, t] - b * coef_ref[3, t])
                        if t == 0:
                            en_ref[f, 2 * l:2 * l + 2] = (yt * coef_ref[0, t] - b * coef_ref[1, t])[0:2]
                        if t == nt - 1:
                            es_ref[f, 2 * l:2 * l + 2] = (yt * coef_ref[0, t] - b * coef_ref[1, t])[6:8]
                made = jnp.concatenate(made, axis=0).astype(BF16)
                l = l0 + 4 * q
                a_ref[f, l:l + 4] = made.reshape(4, rows, 128)
        return gram + gram_of(a_ref[f].reshape(-1, 128))

    g_ref[...] = lax.fori_loop(0, m_ref.shape[0], field, jnp.zeros((128, 128), F32))


def pack(g):
    lane = lax.broadcasted_iota(jnp.int32, (32, 128), 1)
    middle = jnp.where(lane < 32, pltpu.roll(g[96:128], 32, 1), g[32:64])
    last = jnp.where(lane[:16] < 64, pltpu.roll(g[80:96], 64, 1), g[64:80])
    return jnp.concatenate([g[0:32], middle, last], axis=0)


def unpack(p):
    upper = jnp.concatenate([p[0:80], pltpu.roll(p[64:80], 64, 1), pltpu.roll(p[32:64], 96, 1)], axis=0)
    row = lax.broadcasted_iota(jnp.int32, (128, 128), 0)
    col = lax.broadcasted_iota(jnp.int32, (128, 128), 1)
    return jnp.where(col >= row, upper, upper.T)


def outer_kernel(place_ref, en_ref, es_ref, m_ref, lon_a_ref, lon_b_ref, lat_a_ref, lat_b_ref, corner_a_ref,
                 corner_b_ref, bg_ref, gin_ref, an_ref, as_ref, ac_ref, g_ref, pad_ref, x_ref, *, nlat):
    fields, pairs = lat_a_ref.shape[0], lat_a_ref.shape[1]
    rows, cols = bg_ref.shape[1], bg_ref.shape[2]
    first = place_ref[1] * rows
    lon_even = lax.rem(place_ref[0], 2) == 0
    lat_even = lax.rem(place_ref[1], 2) == 0
    has_north, has_south = first > 0, first + rows < nlat
    nt = rows // 8
    sub = sublane()
    gram = gin_ref[...]
    where = lax.broadcasted_iota(jnp.int32, (pairs, 128), 0)
    inside = (where >= 4) & (where < pairs - 4)

    def splat(row):
        return jnp.full((8, 128), row, jnp.int32)

    for e_ref, a_h_ref, b_h_ref, a_c_ref, b_c_ref, use_b, exists, out_ref, near, halo, par, sign, at in (
            (en_ref, lat_a_ref, lat_b_ref, corner_a_ref, corner_b_ref, lat_even, has_north, an_ref, 0, -1, 0, 1, rows + 6),
            (es_ref, lat_b_ref, lat_a_ref, corner_b_ref, corner_a_ref, lat_even, has_south, as_ref, rows - 1, rows, 1, -1,
             rows)):
        c0, k0, _ = scaled_coefs(splat(first + near), nlat)
        c1, k1, _ = scaled_coefs(splat(first + halo), nlat)
        _, _, wa = scaled_coefs(splat(first + near) + (sub % 2 - par), nlat)
        many = pairs // 8
        c = jnp.concatenate([c0 + c1] * many, axis=0)
        k = jnp.concatenate([k0 + k1] * many, axis=0)
        w = jnp.concatenate([0.04 * wa] * many, axis=0)
        outermost = where % 2 == par
        for f in range(fields):
            h = jnp.where(use_b, b_h_ref[f].astype(F32), a_h_ref[f].astype(F32))
            h = jnp.where(exists, h, 0.0)
            pad_ref[8:8 + pairs] = h
            nearer = pad_ref[8 + sign:8 + sign + pairs]
            wide = pad_ref[8 + sign - 2:8 + sign - 2 + pairs] + pad_ref[8 + sign + 2:8 + sign + 2 + pairs]
            more = h + jnp.where(outermost, c * nearer + k * wide, 0.0)
            made = jnp.where(inside, e_ref[f] + w * more, 0.0).astype(BF16)
            out_ref[f] = made
            gram = gram + gram_of(made)
            for l in range(4):
                x_ref[f, 2 + l, at:at + 2] = h[2 * l:2 * l + 2]
                x_ref[f, 6 + l, at:at + 2] = h[pairs - 8 + 2 * l:pairs - 6 + 2 * l]
            corner = jnp.where(use_b, b_c_ref[f].astype(F32), a_c_ref[f].astype(F32))
            corner = jnp.where(exists, corner, 0.0)
            west = jnp.where(lon_even, corner[4:8], corner[0:4])
            east = jnp.where(lon_even, corner[0:4], corner[4:8])
            for l in range(2):
                x_ref[f, l, at:at + 2] = west[2 * l:2 * l + 2]
                x_ref[f, 10 + l, at:at + 2] = east[2 * l:2 * l + 2]
    for f in range(fields):
        for l in range(12):
            x_ref[f, l, rows + 2:rows + 6] = jnp.zeros((4, 128), F32)
        for l in range(4):
            x_ref[f, 2 + l, 0:rows] = m_ref[f, l].astype(F32)
            x_ref[f, 6 + l, 0:rows] = m_ref[f, cols - 4 + l].astype(F32)
        for l in range(2):
            a, b = lon_a_ref[f, l].astype(F32), lon_b_ref[f, l].astype(F32)
            x_ref[f, l, 0:rows] = jnp.where(lon_even, b, a)
            x_ref[f, 10 + l, 0:rows] = jnp.where(lon_even, a, b)

    coefs = [scaled_coefs(first + 8 * t + sub, nlat) for t in range(nt)]
    beyond = first + rows + jnp.where(sub < 4, sub, sub - 8 - rows)
    c, k, _ = scaled_coefs(beyond, nlat)
    real = (beyond >= 0) & (beyond < nlat)
    vc = [x[0] for x in coefs] + [jnp.where(real, c, 0.0)]
    vk = [x[1] for x in coefs] + [jnp.where(real, k, 0.0)]
    one = jnp.where(real, 1.0, 0.0)
    for f in range(fields):
        bg = bg_ref[f].astype(F32)
        for side in range(2):
            u = [tiles_of(x_ref[f, 6 * side + l]) for l in range(6)]
            v = []
            for l in range(1, 5):
                ns = neighbours(u[l], pltpu.roll(u[l][nt], 1, 0), pltpu.roll(u[l][0], 7, 0))
                ns[nt] = one * ns[nt]
                v.append([ns[t] + vc[t] * u[l][t] + vk[t] * (u[l - 1][t] + u[l + 1][t]) for t in range(nt + 1)])
            for l in range(2):
                ns = neighbours(v[l + 1], pltpu.roll(v[l + 1][nt], 1, 0), pltpu.roll(v[l + 1][0], 7, 0))
                at = l + side * (cols - 2)
                parts = []
                for t in range(nt):
                    y = ns[t] + vc[t] * v[l + 1][t] + vk[t] * (v[l][t] + v[l + 2][t])
                    b = jnp.broadcast_to(bg[8 * t:8 * t + 8, at:at + 1], TILE)
                    parts.append((0.04 * y - b) * coefs[t][2])
                ac_ref[f, 2 * side + l] = jnp.concatenate(parts, axis=0).astype(BF16)
    gram = gram + gram_of(ac_ref[...].reshape(-1, 128))
    g_ref[...] = pack(gram)


def factor(g):
    n = 128
    lane = lax.broadcasted_iota(jnp.int32, (8, n), 1)
    sub = lax.broadcasted_iota(jnp.int32, (8, n), 0)
    w = list(g)
    tiles = len(w)
    for b0 in range(tiles):
        cols = [[jnp.broadcast_to(w[b][:, 8 * b0 + j:8 * b0 + j + 1], (8, n)) for b in range(b0, tiles)]
                for j in range(8)]
        for s in range(8):
            k = 8 * b0 + s
            inverse = 1.0 / jnp.broadcast_to(cols[s][0][s:s + 1], (8, n))
            pivot_row = jnp.where(lane == k, 1.0, jnp.broadcast_to(w[b0][s:s + 1], (8, n)))
            rows = [jnp.broadcast_to(cols[j][0][s:s + 1], (8, n)) for j in range(s + 1, 8)]
            for b in range(b0, tiles):
                i = b - b0
                f = cols[s][i] * inverse
                if i == 0:
                    if s == 7:
                        continue
                    f = jnp.where(sub > s, f, 0.0)
                    kept = jnp.where((lane == k) & (sub > s), 0.0, w[b])
                else:
                    kept = jnp.where(lane == k, 0.0, w[b])
                w[b] = kept - f * pivot_row
                for j in range(s + 1, 8):
                    cols[j][i] = cols[j][i] - f * rows[j - s - 1]
    r, x = [], []
    for b in range(tiles):
        diag = lane == sub + 8 * b
        scale = lax.rsqrt(jnp.sum(jnp.where(diag, w[b], 0.0), axis=1, keepdims=True))
        r.append(jnp.where(lane >= sub + 8 * b, w[b] * scale, 0.0))
        x.append(jnp.where(diag, scale, jnp.where(lane < sub + 8 * b, w[b] * scale, 0.0)))
    return jnp.concatenate(r, axis=0), jnp.concatenate(x, axis=0)


def modes_kernel(p_ref, an_ref, as_ref, ac_ref, a_ref, out_hbm, r_ref, x_ref, o_ref, sems, *, total, lons):
    fields, cols, rows, width = out_hbm.shape
    per = cols // lons
    g = unpack(p_ref[...]) * (1.0 / total)
    r, x = factor(tiles_of(g))
    r_ref[...] = r
    inv = x.T
    high = inv.astype(BF16)
    x_ref[0:width] = high
    x_ref[width:] = (inv - high.astype(F32)).astype(BF16)

    def times(a):
        return jnp.dot(jnp.concatenate([a, a], axis=1), x_ref[...], preferred_element_type=F32)

    def part_copy(f, q):
        part = pl.ds(q * lons, lons)
        return pltpu.make_async_copy(o_ref.at[f, part], out_hbm.at[f, part], sems.at[f * per + q])

    for f in range(fields):
        for q in range(per):
            at = slice(q * lons, q * lons + lons)
            o_ref[f, at] = times(a_ref[f, at].reshape(-1, width)).reshape(lons, rows, width)
            north = times(an_ref[f, 2 * q * lons:2 * (q + 1) * lons])
            south = times(as_ref[f, 2 * q * lons:2 * (q + 1) * lons])
            for l in range(lons):
                at = q * lons + l
                if at < 2 or at >= cols - 2:
                    o_ref[f, at] = times(ac_ref[f, at if at < 2 else at - cols + 4])
                else:
                    o_ref[f, at, 0:2] = north[2 * l:2 * l + 2]
                    o_ref[f, at, rows - 2:rows] = south[2 * l:2 * l + 2]
            part_copy(f, q).start()
    for f in range(fields):
        for q in range(per):
            part_copy(f, q).wait()


def exchanges(lon, lat):
    def device(k, z):
        return k * lat + z

    lon_a = [(k, k ^ 1) for k in range(lon)]
    lon_b = [(k, (k - 1 if k % 2 == 0 else k + 1) % lon) for k in range(lon)]
    lat_a = [(device(k, z), device(k, z ^ 1)) for k in range(lon) for z in range(lat)]
    lat_b = []
    for k in range(lon):
        for z in range(lat):
            to = z - 1 if z % 2 == 0 else z + 1
            lat_b.append((device(k, z), device(k, to) if 0 <= to < lat else device(k ^ 1, z)))
    return lon_a, lon_b, lat_a, lat_b


def halos(lon_a, lon_b, lat_a, lat_b):
    lon, lat = lax.axis_size("lon"), lax.axis_size("lat")
    by_lon_a, by_lon_b, by_lat_a, by_lat_b = exchanges(lon, lat)
    both = ("lon", "lat")
    fields, _, rows, width = lon_a.shape
    lat_b = lax.ppermute(lat_b, both, by_lat_b)
    lat_a = lax.ppermute(lat_a, both, by_lat_a)
    lon_b = lax.ppermute(lon_b, "lon", by_lon_b)
    lon_a = lax.ppermute(lon_a, "lon", by_lon_a)
    sides = jnp.concatenate([lon_a, lon_b], axis=1)
    low = sides[:, :, :2].reshape(fields, 8, width)
    high = sides[:, :, rows - 2:].reshape(fields, 8, width)
    even = lax.axis_index("lat") % 2 == 0
    corner_b = lax.ppermute(jnp.where(even, low, high), both, by_lat_b)
    corner_a = lax.ppermute(jnp.where(even, high, low), both, by_lat_a)
    return lon_a, lon_b, lat_a, lat_b, corner_a, corner_b


def total_gram(gram):
    lon, lat = lax.axis_size("lon"), lax.axis_size("lat")

    def partner(dk, dz):
        pairs = [(k * lat + z, (k ^ dk) * lat + (z ^ dz)) for k in range(lon) for z in range(lat)]
        return lax.ppermute(gram, ("lon", "lat"), pairs)

    gram = gram + partner(1, 0)
    by_lon = [1 << i for i in range(1, lon.bit_length() - 1)]
    by_lat = [1 << i for i in range(lat.bit_length() - 1)]
    while by_lon or by_lat:
        if by_lon and by_lat:
            dk, dz = by_lon.pop(0), by_lat.pop(0)
            x, z, xz = partner(dk ^ 1, 0), partner(1, dz), partner(dk ^ 1, dz)
            gram = (gram + x) + (z + xz)
        elif by_lon:
            gram = gram + partner(by_lon.pop(0) ^ 1, 0)
        else:
            gram = gram + partner(1, by_lat.pop(0))
    return gram


def local(members, background):
    fields, rows, cols, width = members.shape
    lat, lon = lax.axis_size("lat"), lax.axis_size("lon")
    nlat = rows * lat
    lons = cols // 4
    pairs = 2 * cols
    place = jnp.stack([lax.axis_index("lon"), lax.axis_index("lat")]).astype(jnp.int32)
    smem = pl.BlockSpec(memory_space=pltpu.SMEM)
    vmem = pl.BlockSpec(memory_space=pltpu.VMEM)
    hbm = pl.BlockSpec(memory_space=pl.ANY)
    params = pltpu.CompilerParams(vmem_limit_bytes=VMEM_LIMIT)

    def kept(*xs):
        return [pltpu.with_memory_space_constraint(x, pltpu.VMEM) for x in xs]

    m, *sent = pl.pallas_call(
        fetch_kernel,
        out_shape=(pltpu.VMEM((fields, cols, rows, width), BF16),) + (pltpu.VMEM((fields, 2, rows, width), BF16),) * 2
        + (pltpu.VMEM((fields, pairs, width), BF16),) * 2,
        in_specs=[smem, hbm],
        out_specs=(vmem,) * 5,
        scratch_shapes=[pltpu.VMEM((pairs, width), F32), pltpu.VMEM((pairs, width), F32),
                        pltpu.SemaphoreType.DMA((fields,))],
        compiler_params=params,
    )(place, pltpu.with_memory_space_constraint(jnp.transpose(members, (0, 2, 1, 3)), pltpu.HBM))
    beside = halos(*sent)
    a, en, es, gram = pl.pallas_call(
        functools.partial(inner_kernel, nlat=nlat),
        out_shape=(pltpu.VMEM((fields, cols, rows, width), BF16), pltpu.VMEM((fields, pairs, width), F32),
                   pltpu.VMEM((fields, pairs, width), F32), pltpu.VMEM((width, width), F32)),
        in_specs=[smem, vmem, vmem],
        out_specs=(vmem,) * 4,
        scratch_shapes=[pltpu.VMEM((256, 256), BF16), pltpu.VMEM((4, rows // 8, 8, 128), F32),
                        pltpu.VMEM((256, 256), F32)],
        compiler_params=params,
        cost_estimate=pl.CostEstimate(flops=16 * fields * cols * rows * width * width,
                                      bytes_accessed=8 * fields * cols * rows * width, transcendentals=0),
    )(place, *kept(m), background)
    an, as_, ac, packed = pl.pallas_call(
        functools.partial(outer_kernel, nlat=nlat),
        out_shape=(pltpu.VMEM((fields, pairs, width), BF16), pltpu.VMEM((fields, pairs, width), BF16),
                   pltpu.VMEM((fields, 4, rows, width), BF16), pltpu.VMEM((80, width), F32)),
        in_specs=[smem] + [vmem] * 11,
        out_specs=(vmem,) * 4,
        scratch_shapes=[pltpu.VMEM((pairs + 16, width), F32), pltpu.VMEM((fields, 12, rows + 8, width), F32)],
        compiler_params=params,
    )(place, *kept(en, es, m, *beside, background, gram))
    packed = total_gram(packed)
    modes, r_factor = pl.pallas_call(
        functools.partial(modes_kernel, total=float(fields * nlat * cols * lon), lons=lons),
        out_shape=(jax.ShapeDtypeStruct((fields, cols, rows, width), F32),
                   jax.ShapeDtypeStruct((width, width), F32)),
        in_specs=[vmem] * 5,
        out_specs=(hbm, vmem),
        scratch_shapes=[pltpu.VMEM((2 * width, width), BF16), pltpu.VMEM((fields, cols, rows, width), F32),
                        pltpu.SemaphoreType.DMA((fields * 4,))],
        compiler_params=params,
    )(*kept(packed, an, as_, ac, a))
    return jnp.transpose(modes, (0, 2, 1, 3)), r_factor


def solution(mesh):
    return jax.shard_map(
        local,
        mesh=mesh,
        in_specs=(P(None, "lat", "lon", None), P(None, "lat", "lon")),
        out_specs=(P(None, "lat", "lon", None), P()),
        check_vma=False,
    )
```

```python
import functools
import math

import jax
import jax.numpy as jnp
from jax import lax
from jax.experimental import pallas as pl
from jax.experimental.pallas import tpu as pltpu
from jax.sharding import PartitionSpec as P

VMEM_LIMIT = 32 * 1024 * 1024
F32 = jnp.float32
BF16 = jnp.bfloat16
TILE = (8, 128)


def row_coefs(glob, nlat):
    phi = (0.125 * (glob.astype(F32) + 0.5) - 0.0625 * nlat) * (math.pi / 180.0)
    square = phi * phi
    cosine = 0.0
    for power in range(14, -2, -2):
        cosine = cosine * square + (-1.0) ** (power // 2) / math.factorial(power)
    return 0.05 + 0.2 * (1.0 - cosine), jnp.sqrt(cosine)


def scaled_coefs(glob, nlat):
    kx, weight = row_coefs(glob, nlat)
    return 3.0 - 10.0 * kx, 5.0 * kx, weight


def sublane():
    return lax.broadcasted_iota(jnp.int32, TILE, 0)


def tiles_of(x):
    return [x[8 * t:8 * t + 8] for t in range(x.shape[0] // 8)]


def neighbours(x, above, below):
    sub = sublane()
    down = [pltpu.roll(t, 1, 0) for t in x]
    up = [pltpu.roll(t, 7, 0) for t in x]
    out = []
    for i in range(len(x)):
        north = jnp.where(sub == 0, down[i - 1] if i else above, down[i])
        south = jnp.where(sub == 7, up[i + 1] if i + 1 < len(x) else below, up[i])
        out.append(north + south)
    return out


def gram_of(a):
    return lax.dot_general(a, a, (((0,), (0,)), ((), ())), preferred_element_type=F32)


def edges_kernel(place_ref, m_hbm, near_ref, lon_a_ref, lon_b_ref, lat_a_ref, lat_b_ref, m_ref, low_ref, high_ref, sems):
    fields, cols, rows, width = m_ref.shape
    lon_even = lax.rem(place_ref[0], 2) == 0
    lat_even = lax.rem(place_ref[1], 2) == 0
    copies = [pltpu.make_async_copy(m_hbm.at[f], m_ref.at[f], sems.at[f]) for f in range(fields)]
    for copy in copies:
        copy.start()
    for f in range(fields):
        copies[f].wait()
        first, last = m_ref[f, 0:2], m_ref[f, cols - 2:cols]
        near_ref[f, 0:4] = m_ref[f, 0:4]
        near_ref[f, 4:8] = m_ref[f, cols - 4:cols]
        lon_a_ref[f] = jnp.where(lon_even, last, first)
        lon_b_ref[f] = jnp.where(lon_even, first, last)
        for l in range(cols):
            low_ref[2 * l:2 * l + 2] = m_ref[f, l, 0:16].astype(F32)[0:2]
            high_ref[2 * l:2 * l + 2] = m_ref[f, l, rows - 16:rows].astype(F32)[14:16]
        low, high = low_ref[...], high_ref[...]
        lat_a_ref[f] = jnp.where(lat_even, high, low).astype(BF16)
        lat_b_ref[f] = jnp.where(lat_even, low, high).astype(BF16)


def inner_kernel(place_ref, m_hbm, bg_ref, a_ref, en_ref, es_ref, g_ref, m_ref, mat_ref, coef_ref, entries_ref, sems, *,
                 nlat):
    cols, rows = m_ref.shape[1], m_ref.shape[2]
    wide = 2
    nt = rows // 8

    def fetch(f):
        return pltpu.make_async_copy(m_hbm.at[f], m_ref.at[f], sems.at[f])

    for f in range(m_ref.shape[0]):
        fetch(f).start()
    first = place_ref[1] * rows

    sub = sublane()
    lane = lax.broadcasted_iota(jnp.int32, TILE, 1)
    for t in range(nt):
        row = 8 * t + sub
        glob = first + row
        c, k, w = scaled_coefs(glob, nlat)
        cn, kn, _ = scaled_coefs(glob - 1, nlat)
        cs, ks, _ = scaled_coefs(glob + 1, nlat)
        live = (row >= 2) & (row < rows - 2)
        coef_ref[0, t], coef_ref[1, t] = 0.04 * w, w
        coef_ref[2, t], coef_ref[3, t] = jnp.where(live, 0.04 * w, 0.0), jnp.where(live, w, 0.0)
        both = jnp.where((glob == 0) | (glob == nlat - 1), 1.0, 2.0)
        dj = lax.rem(lane, rows) - row
        for i in range(4):
            for half in range(2):
                dl = jnp.abs(4 * half + lax.div(lane, rows) - i - 2)
                by_lon = lambda zero, one, two: jnp.where(
                    dl == 0, zero, jnp.where(dl == 1, one, jnp.where(dl == 2, two, 0.0)))
                entry = jnp.where(
                    dj == 0, by_lon(both + c * c + 2.0 * k * k, 2.0 * c * k, k * k), jnp.where(
                        dj == -1, by_lon(c + cn, k + kn, 0.0), jnp.where(
                            dj == 1, by_lon(c + cs, k + ks, 0.0), jnp.where(
                                (jnp.abs(dj) == 2) & (dl == 0), 1.0, 0.0))))
                high = entry.astype(BF16).astype(F32)
                at = pl.ds(rows * i + 8 * t, 8), pl.ds(128 * half, 128)
                entries_ref[at[0], at[1]] = high
                entries_ref[pl.ds(128 + rows * i + 8 * t, 8), at[1]] = entry - high
    mat_ref[...] = entries_ref[...].astype(BF16)

    @pl.loop(0, m_ref.shape[0])
    def _(f):
        fetch(f).wait()
        ground = bg_ref[f].astype(F32)
        for l in (0, 1, cols - 2, cols - 1):
            a_ref[f, l] = jnp.zeros((rows, 128), BF16)
        for l0 in range(2, cols - 2, 4 * wide):
            chunk = [m_ref[f, l - 2:l + 6].reshape(256, 128) for l in range(l0, min(l0 + 4 * wide, cols - 2), 4)]
            y = jnp.dot(mat_ref[...], jnp.concatenate(chunk, axis=1), preferred_element_type=F32)
            y = y[:128] + y[128:]
            for q in range(len(chunk)):
                made = []
                for i in range(4):
                    l = l0 + 4 * q + i
                    for t in range(nt):
                        yt = y[rows * i + 8 * t:rows * i + 8 * t + 8, 128 * q:128 * q + 128]
                        b = jnp.broadcast_to(ground[8 * t:8 * t + 8, l:l + 1], TILE)
                        made.append(yt * coef_ref[2, t] - b * coef_ref[3, t])
                        if t == 0:
                            en_ref[f, 2 * l:2 * l + 2] = (yt * coef_ref[0, t] - b * coef_ref[1, t])[0:2]
                        if t == nt - 1:
                            es_ref[f, 2 * l:2 * l + 2] = (yt * coef_ref[0, t] - b * coef_ref[1, t])[6:8]
                made = jnp.concatenate(made, axis=0).astype(BF16)
                l = l0 + 4 * q
                a_ref[f, l:l + 4] = made.reshape(4, rows, 128)

    g_ref[...] = gram_of(a_ref[...].reshape(-1, 128))


def pack(g):
    lane = lax.broadcasted_iota(jnp.int32, (32, 128), 1)
    middle = jnp.where(lane < 32, pltpu.roll(g[96:128], 32, 1), g[32:64])
    last = jnp.where(lane[:16] < 64, pltpu.roll(g[80:96], 64, 1), g[64:80])
    return jnp.concatenate([g[0:32], middle, last], axis=0)


def unpack(p):
    upper = jnp.concatenate([p[0:80], pltpu.roll(p[64:80], 64, 1), pltpu.roll(p[32:64], 96, 1)], axis=0)
    row = lax.broadcasted_iota(jnp.int32, (128, 128), 0)
    col = lax.broadcasted_iota(jnp.int32, (128, 128), 1)
    return jnp.where(col >= row, upper, upper.T)


def outer_kernel(place_ref, en_ref, es_ref, near_ref, lon_a_ref, lon_b_ref, lat_a_ref, lat_b_ref, corner_a_ref,
                 corner_b_ref, bg_ref, gin_ref, an_ref, as_ref, ac_ref, g_ref, pad_ref, x_ref, *, nlat):
    fields, pairs = lat_a_ref.shape[0], lat_a_ref.shape[1]
    rows, cols = bg_ref.shape[1], bg_ref.shape[2]
    first = place_ref[1] * rows
    lon_even = lax.rem(place_ref[0], 2) == 0
    lat_even = lax.rem(place_ref[1], 2) == 0
    has_north, has_south = first > 0, first + rows < nlat
    nt = rows // 8
    sub = sublane()
    gram = gin_ref[...]

    def splat(row):
        return jnp.full((8, 128), row, jnp.int32)

    for e_ref, a_h_ref, b_h_ref, a_c_ref, b_c_ref, use_b, exists, out_ref, near, halo, par, sign, at in (
            (en_ref, lat_a_ref, lat_b_ref, corner_a_ref, corner_b_ref, lat_even, has_north, an_ref, 0, -1, 0, 1, rows + 6),
            (es_ref, lat_b_ref, lat_a_ref, corner_b_ref, corner_a_ref, lat_even, has_south, as_ref, rows - 1, rows, 1, -1,
             rows)):
        c0, k0, _ = scaled_coefs(splat(first + near), nlat)
        c1, k1, _ = scaled_coefs(splat(first + halo), nlat)
        _, _, wa = scaled_coefs(splat(first + near) + (sub % 2 - par), nlat)
        many = pairs // 8
        outermost = sub % 2 == par
        c = jnp.concatenate([jnp.where(outermost, c0 + c1, 0.0)] * many, axis=0)
        k = jnp.concatenate([jnp.where(outermost, k0 + k1, 0.0)] * many, axis=0)
        w = jnp.concatenate([jnp.where(exists, 0.04 * wa, 0.0)] * many, axis=0)
        for f in range(fields):
            h = jnp.where(use_b, b_h_ref[f], a_h_ref[f]).astype(F32)
            pad = pad_ref.at[fields * par + f]
            pad[8:8 + pairs] = h
            nearer = pad[8 + sign:8 + sign + pairs]
            wide = pad[8 + sign - 2:8 + sign - 2 + pairs] + pad[8 + sign + 2:8 + sign + 2 + pairs]
            made = e_ref[f] + w * (h + c * nearer + k * wide)
            made = jnp.concatenate([jnp.where(sub >= 4, made[:8], 0.0), made[8:pairs - 8],
                                    jnp.where(sub < 4, made[pairs - 8:], 0.0)], axis=0).astype(BF16)
            edge = jnp.where(exists, jnp.concatenate([h[:8], h[pairs - 8:]], axis=0), 0.0)
            out_ref[f] = made
            gram = gram + gram_of(made)
            for l in range(4):
                x_ref[f, 2 + l, at:at + 2] = edge[2 * l:2 * l + 2]
                x_ref[f, 6 + l, at:at + 2] = edge[8 + 2 * l:10 + 2 * l]
            corner = jnp.where(use_b, b_c_ref[f].astype(F32), a_c_ref[f].astype(F32))
            corner = jnp.where(exists, corner, 0.0)
            west = jnp.where(lon_even, corner[4:8], corner[0:4])
            east = jnp.where(lon_even, corner[0:4], corner[4:8])
            for l in range(2):
                x_ref[f, l, at:at + 2] = west[2 * l:2 * l + 2]
                x_ref[f, 10 + l, at:at + 2] = east[2 * l:2 * l + 2]
    for f in range(fields):
        for l in range(12):
            x_ref[f, l, rows + 2:rows + 6] = jnp.zeros((4, 128), F32)
        for l in range(4):
            x_ref[f, 2 + l, 0:rows] = near_ref[f, l].astype(F32)
            x_ref[f, 6 + l, 0:rows] = near_ref[f, 4 + l].astype(F32)
        for l in range(2):
            a, b = lon_a_ref[f, l].astype(F32), lon_b_ref[f, l].astype(F32)
            x_ref[f, l, 0:rows] = jnp.where(lon_even, b, a)
            x_ref[f, 10 + l, 0:rows] = jnp.where(lon_even, a, b)

    coefs = [scaled_coefs(first + 8 * t + sub, nlat) for t in range(nt)]
    beyond = first + rows + jnp.where(sub < 4, sub, sub - 8 - rows)
    c, k, _ = scaled_coefs(beyond, nlat)
    real = (beyond >= 0) & (beyond < nlat)
    vc = [x[0] for x in coefs] + [jnp.where(real, c, 0.0)]
    vk = [x[1] for x in coefs] + [jnp.where(real, k, 0.0)]
    one = jnp.where(real, 1.0, 0.0)
    for f in range(fields):
        bg = bg_ref[f].astype(F32)
        for side in range(2):
            u = [tiles_of(x_ref[f, 6 * side + l]) for l in range(6)]
            v = []
            for l in range(1, 5):
                ns = neighbours(u[l], pltpu.roll(u[l][nt], 1, 0), pltpu.roll(u[l][0], 7, 0))
                ns[nt] = one * ns[nt]
                v.append([ns[t] + vc[t] * u[l][t] + vk[t] * (u[l - 1][t] + u[l + 1][t]) for t in range(nt + 1)])
            for l in range(2):
                ns = neighbours(v[l + 1], pltpu.roll(v[l + 1][nt], 1, 0), pltpu.roll(v[l + 1][0], 7, 0))
                at = l + side * (cols - 2)
                parts = []
                for t in range(nt):
                    y = ns[t] + vc[t] * v[l + 1][t] + vk[t] * (v[l][t] + v[l + 2][t])
                    b = jnp.broadcast_to(bg[8 * t:8 * t + 8, at:at + 1], TILE)
                    parts.append((0.04 * y - b) * coefs[t][2])
                ac_ref[f, 2 * side + l] = jnp.concatenate(parts, axis=0).astype(BF16)
    gram = gram + gram_of(ac_ref[...].reshape(-1, 128))
    g_ref[...] = pack(gram)


def factor(g):
    n, block, near = 128, 16, 4
    lane = lax.broadcasted_iota(jnp.int32, (8, n), 1)
    sub = sublane()
    w = list(g)
    for t0 in range(0, len(w), 2):
        k0 = 8 * t0
        close = range(t0, min(len(w), t0 + near))
        cols = {b: [jnp.broadcast_to(w[b][:, k0 + j:k0 + j + 1], (8, n)) for j in range(block)] for b in close}
        below = {b: jnp.where((lane >= k0) & (lane < k0 + block), 0.0, w[b]) for b in range(t0 + 2, len(w))}
        inverses = [None, None]
        for s in range(block):
            k, top, row = k0 + s, t0 + s // 8, s % 8
            inverse = 1.0 / jnp.broadcast_to(cols[top][s][row:row + 1], (8, n))
            old = inverses[s // 8]
            inverses[s // 8] = inverse if old is None else jnp.where(sub >= row, inverse, old)
            pivot_row = jnp.where(lane == k, 1.0, jnp.broadcast_to(w[top][row:row + 1], (8, n)))
            outside = jnp.where((lane > k) & (lane < k0 + block), 0.0, pivot_row)
            heads = [jnp.broadcast_to(cols[top][j][row:row + 1], (8, n)) for j in range(s + 1, block)]
            for b in close:
                if b < top or (b == top and row == 7):
                    continue
                f = cols[b][s] * inverse
                if b == top:
                    f = jnp.where(sub > row, f, 0.0)
                if b < t0 + 2:
                    at = (lane == k) & (sub > row) if b == top else lane == k
                    w[b] = jnp.where(at, 0.0, w[b]) - f * pivot_row
                else:
                    below[b] = below[b] - f * outside
                for j in range(s + 1, block):
                    cols[b][j] = cols[b][j] - f * heads[j - s - 1]
        if t0 + near < len(w):
            factors, rows = [], []
            for h in range(2):
                pivot = k0 + 8 * h + sub
                factors.append(w[t0 + h] * inverses[h])
                rows.append(jnp.where(lane == pivot, 1.0,
                                      jnp.where((lane > pivot) & (lane < k0 + block), 0.0, w[t0 + h])))
            update = lax.dot_general(jnp.concatenate(factors, axis=0), jnp.concatenate(rows, axis=0),
                                     (((0,), (0,)), ((), ())), precision=lax.Precision.HIGHEST,
                                     preferred_element_type=F32)
            for b in range(t0 + near, len(w)):
                below[b] = below[b] - update[8 * b:8 * b + 8]
        for b in below:
            w[b] = below[b]
    r, x = [], []
    for b in range(len(w)):
        diag = lane == sub + 8 * b
        scale = lax.rsqrt(jnp.sum(jnp.where(diag, w[b], 0.0), axis=1, keepdims=True))
        r.append(jnp.where(lane >= sub + 8 * b, w[b] * scale, 0.0))
        x.append(jnp.where(diag, scale, jnp.where(lane < sub + 8 * b, w[b] * scale, 0.0)))
    return jnp.concatenate(r, axis=0), jnp.concatenate(x, axis=0)


def modes_kernel(p_ref, an_ref, as_ref, ac_ref, a_ref, out_hbm, r_ref, x_ref, o_ref, sems, *, total):
    fields, cols, rows, width = out_hbm.shape
    quarter = cols // 4
    bounds = [quarter * q for q in range(5)]
    parts = [(f, lo, hi) for f in range(fields) for lo, hi in zip(bounds, bounds[1:])]
    parts[:1] = [(0, 0, quarter // 3), (0, quarter // 3, quarter)]
    g = unpack(p_ref[...]) * (1.0 / total)
    r, x = factor(tiles_of(g))
    r_ref[...] = r
    inv = x.T
    high = inv.astype(BF16)
    x_ref[0:width] = high
    x_ref[width:] = (inv - high.astype(F32)).astype(BF16)

    def times(a):
        return jnp.dot(jnp.concatenate([a, a], axis=1), x_ref[...], preferred_element_type=F32)

    def leave(i):
        f, lo, hi = parts[i]
        return pltpu.make_async_copy(o_ref.at[f, pl.ds(lo, hi - lo)], out_hbm.at[f, pl.ds(lo, hi - lo)], sems.at[i])

    for i, (f, lo, hi) in enumerate(parts):
        o_ref[f, lo:hi] = times(a_ref[f, lo:hi].reshape(-1, width)).reshape(hi - lo, rows, width)
        if lo == 0:
            north, south = times(an_ref[f]), times(as_ref[f])
        for l in range(lo, hi):
            if l < 2 or l >= cols - 2:
                o_ref[f, l] = times(ac_ref[f, l if l < 2 else l - cols + 4])
            else:
                o_ref[f, l, 0:2] = north[2 * l:2 * l + 2]
                o_ref[f, l, rows - 2:rows] = south[2 * l:2 * l + 2]
        leave(i).start()
    for i in range(len(parts)):
        leave(i).wait()


def exchanges(lon, lat):
    def device(k, z):
        return k * lat + z

    lon_a = [(k, k ^ 1) for k in range(lon)]
    lon_b = [(k, (k - 1 if k % 2 == 0 else k + 1) % lon) for k in range(lon)]
    lat_a = [(device(k, z), device(k, z ^ 1)) for k in range(lon) for z in range(lat)]
    lat_b = []
    for k in range(lon):
        for z in range(lat):
            to = z - 1 if z % 2 == 0 else z + 1
            lat_b.append((device(k, z), device(k, to) if 0 <= to < lat else device(k ^ 1, z)))
    return lon_a, lon_b, lat_a, lat_b


def halos(lon_a, lon_b, lat_a, lat_b):
    lon, lat = lax.axis_size("lon"), lax.axis_size("lat")
    by_lon_a, by_lon_b, by_lat_a, by_lat_b = exchanges(lon, lat)
    both = ("lon", "lat")
    fields, _, rows, width = lon_a.shape
    lat_b = lax.ppermute(lat_b, both, by_lat_b)
    lat_a = lax.ppermute(lat_a, both, by_lat_a)
    lon_b = lax.ppermute(lon_b, "lon", by_lon_b)
    lon_a = lax.ppermute(lon_a, "lon", by_lon_a)
    sides = jnp.concatenate([lon_a, lon_b], axis=1)
    low = sides[:, :, :2].reshape(fields, 8, width)
    high = sides[:, :, rows - 2:].reshape(fields, 8, width)
    even = lax.axis_index("lat") % 2 == 0
    corner_b = lax.ppermute(jnp.where(even, low, high), both, by_lat_b)
    corner_a = lax.ppermute(jnp.where(even, high, low), both, by_lat_a)
    return lon_a, lon_b, lat_a, lat_b, corner_a, corner_b


def total_gram(gram):
    lon, lat = lax.axis_size("lon"), lax.axis_size("lat")

    def partner(dk, dz):
        pairs = [(k * lat + z, (k ^ dk) * lat + (z ^ dz)) for k in range(lon) for z in range(lat)]
        return lax.ppermute(gram, ("lon", "lat"), pairs)

    gram = gram + partner(1, 0)
    by_lon = [1 << i for i in range(1, lon.bit_length() - 1)]
    by_lat = [1 << i for i in range(lat.bit_length() - 1)]
    while by_lon or by_lat:
        if by_lon and by_lat:
            dk, dz = by_lon.pop(0), by_lat.pop(0)
            x, z, xz = partner(dk ^ 1, 0), partner(1, dz), partner(dk ^ 1, dz)
            gram = (gram + x) + (z + xz)
        elif by_lon:
            gram = gram + partner(by_lon.pop(0) ^ 1, 0)
        else:
            gram = gram + partner(1, by_lat.pop(0))
    return gram


def local(members, background):
    fields, rows, cols, width = members.shape
    lat, lon = lax.axis_size("lat"), lax.axis_size("lon")
    nlat = rows * lat
    pairs = 2 * cols
    place = jnp.stack([lax.axis_index("lon"), lax.axis_index("lat")]).astype(jnp.int32)
    smem = pl.BlockSpec(memory_space=pltpu.SMEM)
    vmem = pl.BlockSpec(memory_space=pltpu.VMEM)
    hbm = pl.BlockSpec(memory_space=pl.ANY)
    params = pltpu.CompilerParams(vmem_limit_bytes=VMEM_LIMIT)

    def kept(*xs):
        return [pltpu.with_memory_space_constraint(x, pltpu.VMEM) for x in xs]

    m = pltpu.with_memory_space_constraint(jnp.transpose(members, (0, 2, 1, 3)), pltpu.HBM)
    near, *sent = pl.pallas_call(
        edges_kernel,
        out_shape=(pltpu.VMEM((fields, 8, rows, width), BF16),) + (pltpu.VMEM((fields, 2, rows, width), BF16),) * 2
        + (pltpu.VMEM((fields, pairs, width), BF16),) * 2,
        in_specs=[smem, hbm],
        out_specs=(vmem,) * 5,
        scratch_shapes=[pltpu.VMEM((fields, cols, rows, width), BF16), pltpu.VMEM((pairs, width), F32),
                        pltpu.VMEM((pairs, width), F32), pltpu.SemaphoreType.DMA((fields,))],
        compiler_params=params,
    )(place, m)
    beside = halos(*sent)
    a, en, es, gram = pl.pallas_call(
        functools.partial(inner_kernel, nlat=nlat),
        out_shape=(pltpu.VMEM((fields, cols, rows, width), BF16), pltpu.VMEM((fields, pairs, width), F32),
                   pltpu.VMEM((fields, pairs, width), F32), pltpu.VMEM((width, width), F32)),
        in_specs=[smem, hbm, vmem],
        out_specs=(vmem,) * 4,
        scratch_shapes=[pltpu.VMEM((fields, cols, rows, width), BF16), pltpu.VMEM((256, 256), BF16),
                        pltpu.VMEM((4, rows // 8, 8, 128), F32), pltpu.VMEM((256, 256), F32),
                        pltpu.SemaphoreType.DMA((fields,))],
        compiler_params=params,
        cost_estimate=pl.CostEstimate(flops=16 * fields * cols * rows * width * width,
                                      bytes_accessed=8 * fields * cols * rows * width, transcendentals=0),
    )(place, m, background)
    an, as_, ac, packed = pl.pallas_call(
        functools.partial(outer_kernel, nlat=nlat),
        out_shape=(pltpu.VMEM((fields, pairs, width), BF16), pltpu.VMEM((fields, pairs, width), BF16),
                   pltpu.VMEM((fields, 4, rows, width), BF16), pltpu.VMEM((80, width), F32)),
        in_specs=[smem] + [vmem] * 11,
        out_specs=(vmem,) * 4,
        scratch_shapes=[pltpu.VMEM((2 * fields, pairs + 16, width), F32),
                        pltpu.VMEM((fields, 12, rows + 8, width), F32)],
        compiler_params=params,
    )(place, *kept(en, es, near, *beside, background, gram))
    packed = total_gram(packed)
    modes, r_factor = pl.pallas_call(
        functools.partial(modes_kernel, total=float(fields * nlat * cols * lon)),
        out_shape=(jax.ShapeDtypeStruct((fields, cols, rows, width), F32),
                   jax.ShapeDtypeStruct((width, width), F32)),
        in_specs=[vmem] * 5,
        out_specs=(hbm, vmem),
        scratch_shapes=[pltpu.VMEM((2 * width, width), BF16), pltpu.VMEM((fields, cols, rows, width), F32),
                        pltpu.SemaphoreType.DMA((fields * 4 + 1,))],
        compiler_params=params,
    )(*kept(packed, an, as_, ac, a))
    return jnp.transpose(modes, (0, 2, 1, 3)), r_factor


def solution(mesh):
    return jax.shard_map(
        local,
        mesh=mesh,
        in_specs=(P(None, "lat", "lon", None), P(None, "lat", "lon")),
        out_specs=(P(None, "lat", "lon", None), P()),
        check_vma=False,
    )
```

```python
import functools
import math

import jax
import jax.numpy as jnp
from jax import lax
from jax.experimental import pallas as pl
from jax.experimental.pallas import tpu as pltpu
from jax.sharding import PartitionSpec as P

VMEM_LIMIT = 32 * 1024 * 1024
F32 = jnp.float32
BF16 = jnp.bfloat16
TILE = (8, 128)


def row_coefs(glob, nlat):
    phi = (0.125 * (glob.astype(F32) + 0.5) - 0.0625 * nlat) * (math.pi / 180.0)
    square = phi * phi
    cosine = 0.0
    for power in range(14, -2, -2):
        cosine = cosine * square + (-1.0) ** (power // 2) / math.factorial(power)
    return 0.05 + 0.2 * (1.0 - cosine), jnp.sqrt(cosine)


def scaled_coefs(glob, nlat):
    kx, weight = row_coefs(glob, nlat)
    return 3.0 - 10.0 * kx, 5.0 * kx, weight


def sublane():
    return lax.broadcasted_iota(jnp.int32, TILE, 0)


def tiles_of(x):
    return [x[8 * t:8 * t + 8] for t in range(x.shape[0] // 8)]


def neighbours(x, above, below):
    sub = sublane()
    down = [pltpu.roll(t, 1, 0) for t in x]
    up = [pltpu.roll(t, 7, 0) for t in x]
    out = []
    for i in range(len(x)):
        north = jnp.where(sub == 0, down[i - 1] if i else above, down[i])
        south = jnp.where(sub == 7, up[i + 1] if i + 1 < len(x) else below, up[i])
        out.append(north + south)
    return out


def gram_of(a):
    return lax.dot_general(a, a, (((0,), (0,)), ((), ())), preferred_element_type=F32)


def edges_kernel(place_ref, m_hbm, m_ref, near_ref, even_ref, lon_a_ref, lon_b_ref, lat_a_ref, lat_b_ref, low_ref, high_ref,
                 sems):
    fields, cols, rows, width = m_ref.shape
    lon_even = lax.rem(place_ref[0], 2) == 0
    lat_even = lax.rem(place_ref[1], 2) == 0
    even_ref[...] = jnp.where(jnp.full(even_ref.shape, lat_even, jnp.bool_), 1.0, 0.0)
    copies = [pltpu.make_async_copy(m_hbm.at[f], m_ref.at[f], sems.at[f]) for f in range(fields)]
    for copy in copies:
        copy.start()
    for f in range(fields):
        copies[f].wait()
        first, last = m_ref[f, 0:2], m_ref[f, cols - 2:cols]
        near_ref[f, 0:4] = m_ref[f, 0:4]
        near_ref[f, 4:8] = m_ref[f, cols - 4:cols]
        lon_a_ref[f] = jnp.where(lon_even, last, first)
        lon_b_ref[f] = jnp.where(lon_even, first, last)
        for l in range(cols):
            low_ref[2 * l:2 * l + 2] = m_ref[f, l, 0:16].astype(F32)[0:2]
            high_ref[2 * l:2 * l + 2] = m_ref[f, l, rows - 16:rows].astype(F32)[14:16]
        low, high = low_ref[...], high_ref[...]
        lat_a_ref[f] = jnp.where(lat_even, high, low).astype(BF16)
        lat_b_ref[f] = jnp.where(lat_even, low, high).astype(BF16)


def inner_kernel(place_ref, m_ref, bg_ref, a_ref, en_ref, es_ref, g_ref, mat_ref, coef_ref, entries_ref, *, nlat):
    cols, rows = m_ref.shape[1], m_ref.shape[2]
    wide = 2
    nt = rows // 8
    first = place_ref[1] * rows
    sub = sublane()
    lane = lax.broadcasted_iota(jnp.int32, TILE, 1)
    for t in range(nt):
        row = 8 * t + sub
        glob = first + row
        c, k, w = scaled_coefs(glob, nlat)
        cn, kn, _ = scaled_coefs(glob - 1, nlat)
        cs, ks, _ = scaled_coefs(glob + 1, nlat)
        live = (row >= 2) & (row < rows - 2)
        coef_ref[0, t], coef_ref[1, t] = 0.04 * w, w
        coef_ref[2, t], coef_ref[3, t] = jnp.where(live, 0.04 * w, 0.0), jnp.where(live, w, 0.0)
        both = jnp.where((glob == 0) | (glob == nlat - 1), 1.0, 2.0)
        dj = lax.rem(lane, rows) - row
        for i in range(4):
            for half in range(2):
                dl = jnp.abs(4 * half + lax.div(lane, rows) - i - 2)
                by_lon = lambda zero, one, two: jnp.where(
                    dl == 0, zero, jnp.where(dl == 1, one, jnp.where(dl == 2, two, 0.0)))
                entry = jnp.where(
                    dj == 0, by_lon(both + c * c + 2.0 * k * k, 2.0 * c * k, k * k), jnp.where(
                        dj == -1, by_lon(c + cn, k + kn, 0.0), jnp.where(
                            dj == 1, by_lon(c + cs, k + ks, 0.0), jnp.where(
                                (jnp.abs(dj) == 2) & (dl == 0), 1.0, 0.0))))
                high = entry.astype(BF16).astype(F32)
                at = pl.ds(rows * i + 8 * t, 8), pl.ds(128 * half, 128)
                entries_ref[at[0], at[1]] = high
                entries_ref[pl.ds(128 + rows * i + 8 * t, 8), at[1]] = entry - high
    mat_ref[...] = entries_ref[...].astype(BF16)

    @pl.loop(0, m_ref.shape[0])
    def _(f):
        ground = bg_ref[f].astype(F32)
        for l in (0, 1, cols - 2, cols - 1):
            a_ref[f, l] = jnp.zeros((rows, 128), BF16)
        for l0 in range(2, cols - 2, 4 * wide):
            chunk = [m_ref[f, l - 2:l + 6].reshape(256, 128) for l in range(l0, min(l0 + 4 * wide, cols - 2), 4)]
            y = jnp.dot(mat_ref[...], jnp.concatenate(chunk, axis=1), preferred_element_type=F32)
            y = y[:128] + y[128:]
            for q in range(len(chunk)):
                made = []
                for i in range(4):
                    l = l0 + 4 * q + i
                    for t in range(nt):
                        yt = y[rows * i + 8 * t:rows * i + 8 * t + 8, 128 * q:128 * q + 128]
                        b = jnp.broadcast_to(ground[8 * t:8 * t + 8, l:l + 1], TILE)
                        made.append(yt * coef_ref[2, t] - b * coef_ref[3, t])
                        if t == 0:
                            en_ref[f, 2 * l:2 * l + 2] = (yt * coef_ref[0, t] - b * coef_ref[1, t])[0:2]
                        if t == nt - 1:
                            es_ref[f, 2 * l:2 * l + 2] = (yt * coef_ref[0, t] - b * coef_ref[1, t])[6:8]
                made = jnp.concatenate(made, axis=0).astype(BF16)
                l = l0 + 4 * q
                a_ref[f, l:l + 4] = made.reshape(4, rows, 128)

    g_ref[...] = gram_of(a_ref[...].reshape(-1, 128))


def pack(g):
    lane = lax.broadcasted_iota(jnp.int32, (32, 128), 1)
    middle = jnp.where(lane < 32, pltpu.roll(g[96:128], 32, 1), g[32:64])
    last = jnp.where(lane[:16] < 64, pltpu.roll(g[80:96], 64, 1), g[64:80])
    return jnp.concatenate([g[0:32], middle, last], axis=0)


def unpack(p):
    upper = jnp.concatenate([p[0:80], pltpu.roll(p[64:80], 64, 1), pltpu.roll(p[32:64], 96, 1)], axis=0)
    row = lax.broadcasted_iota(jnp.int32, (128, 128), 0)
    col = lax.broadcasted_iota(jnp.int32, (128, 128), 1)
    return jnp.where(col >= row, upper, upper.T)


def outer_kernel(place_ref, en_ref, es_ref, near_ref, lon_a_ref, lon_b_ref, lat_a_ref, lat_b_ref, corner_a_ref,
                 corner_b_ref, bg_ref, gin_ref, an_ref, as_ref, ac_ref, g_ref, pad_ref, x_ref, *, nlat):
    fields, pairs = lat_a_ref.shape[0], lat_a_ref.shape[1]
    rows, cols = bg_ref.shape[1], bg_ref.shape[2]
    first = place_ref[1] * rows
    lon_even = lax.rem(place_ref[0], 2) == 0
    lat_even = lax.rem(place_ref[1], 2) == 0
    has_north, has_south = first > 0, first + rows < nlat
    nt = rows // 8
    sub = sublane()
    gram = gin_ref[...]

    def splat(row):
        return jnp.full((8, 128), row, jnp.int32)

    for e_ref, a_h_ref, b_h_ref, a_c_ref, b_c_ref, use_b, exists, out_ref, near, halo, par, sign, at in (
            (en_ref, lat_a_ref, lat_b_ref, corner_a_ref, corner_b_ref, lat_even, has_north, an_ref, 0, -1, 0, 1, rows + 6),
            (es_ref, lat_b_ref, lat_a_ref, corner_b_ref, corner_a_ref, lat_even, has_south, as_ref, rows - 1, rows, 1, -1,
             rows)):
        c0, k0, _ = scaled_coefs(splat(first + near), nlat)
        c1, k1, _ = scaled_coefs(splat(first + halo), nlat)
        _, _, wa = scaled_coefs(splat(first + near) + (sub % 2 - par), nlat)
        many = pairs // 8
        outermost = sub % 2 == par
        c = jnp.concatenate([jnp.where(outermost, c0 + c1, 0.0)] * many, axis=0)
        k = jnp.concatenate([jnp.where(outermost, k0 + k1, 0.0)] * many, axis=0)
        w = jnp.concatenate([jnp.where(exists, 0.04 * wa, 0.0)] * many, axis=0)
        for f in range(fields):
            h = jnp.where(use_b, b_h_ref[f], a_h_ref[f]).astype(F32)
            pad = pad_ref.at[fields * par + f]
            pad[8:8 + pairs] = h
            nearer = pad[8 + sign:8 + sign + pairs]
            wide = pad[8 + sign - 2:8 + sign - 2 + pairs] + pad[8 + sign + 2:8 + sign + 2 + pairs]
            made = e_ref[f] + w * (h + c * nearer + k * wide)
            made = jnp.concatenate([jnp.where(sub >= 4, made[:8], 0.0), made[8:pairs - 8],
                                    jnp.where(sub < 4, made[pairs - 8:], 0.0)], axis=0).astype(BF16)
            edge = jnp.where(exists, jnp.concatenate([h[:8], h[pairs - 8:]], axis=0), 0.0)
            out_ref[f] = made
            gram = gram + gram_of(made)
            for l in range(4):
                x_ref[f, 2 + l, at:at + 2] = edge[2 * l:2 * l + 2]
                x_ref[f, 6 + l, at:at + 2] = edge[8 + 2 * l:10 + 2 * l]
            corner = jnp.where(use_b, b_c_ref[f].astype(F32), a_c_ref[f].astype(F32))
            corner = jnp.where(exists, corner, 0.0)
            west = jnp.where(lon_even, corner[4:8], corner[0:4])
            east = jnp.where(lon_even, corner[0:4], corner[4:8])
            for l in range(2):
                x_ref[f, l, at:at + 2] = west[2 * l:2 * l + 2]
                x_ref[f, 10 + l, at:at + 2] = east[2 * l:2 * l + 2]
    for f in range(fields):
        for l in range(12):
            x_ref[f, l, rows + 2:rows + 6] = jnp.zeros((4, 128), F32)
        for l in range(4):
            x_ref[f, 2 + l, 0:rows] = near_ref[f, l].astype(F32)
            x_ref[f, 6 + l, 0:rows] = near_ref[f, 4 + l].astype(F32)
        for l in range(2):
            a, b = lon_a_ref[f, l].astype(F32), lon_b_ref[f, l].astype(F32)
            x_ref[f, l, 0:rows] = jnp.where(lon_even, b, a)
            x_ref[f, 10 + l, 0:rows] = jnp.where(lon_even, a, b)

    coefs = [scaled_coefs(first + 8 * t + sub, nlat) for t in range(nt)]
    beyond = first + rows + jnp.where(sub < 4, sub, sub - 8 - rows)
    c, k, _ = scaled_coefs(beyond, nlat)
    real = (beyond >= 0) & (beyond < nlat)
    vc = [x[0] for x in coefs] + [jnp.where(real, c, 0.0)]
    vk = [x[1] for x in coefs] + [jnp.where(real, k, 0.0)]
    one = jnp.where(real, 1.0, 0.0)
    for f in range(fields):
        bg = bg_ref[f].astype(F32)
        for side in range(2):
            u = [tiles_of(x_ref[f, 6 * side + l]) for l in range(6)]
            v = []
            for l in range(1, 5):
                ns = neighbours(u[l], pltpu.roll(u[l][nt], 1, 0), pltpu.roll(u[l][0], 7, 0))
                ns[nt] = one * ns[nt]
                v.append([ns[t] + vc[t] * u[l][t] + vk[t] * (u[l - 1][t] + u[l + 1][t]) for t in range(nt + 1)])
            for l in range(2):
                ns = neighbours(v[l + 1], pltpu.roll(v[l + 1][nt], 1, 0), pltpu.roll(v[l + 1][0], 7, 0))
                at = l + side * (cols - 2)
                parts = []
                for t in range(nt):
                    y = ns[t] + vc[t] * v[l + 1][t] + vk[t] * (v[l][t] + v[l + 2][t])
                    b = jnp.broadcast_to(bg[8 * t:8 * t + 8, at:at + 1], TILE)
                    parts.append((0.04 * y - b) * coefs[t][2])
                ac_ref[f, 2 * side + l] = jnp.concatenate(parts, axis=0).astype(BF16)
    gram = gram + gram_of(ac_ref[...].reshape(-1, 128))
    g_ref[...] = pack(gram)


def factor(g):
    n, block, near = 128, 16, 4
    lane = lax.broadcasted_iota(jnp.int32, (8, n), 1)
    sub = sublane()
    w = list(g)
    for t0 in range(0, len(w), 2):
        k0 = 8 * t0
        close = range(t0, min(len(w), t0 + near))
        cols = {b: [jnp.broadcast_to(w[b][:, k0 + j:k0 + j + 1], (8, n)) for j in range(block)] for b in close}
        below = {b: jnp.where((lane >= k0) & (lane < k0 + block), 0.0, w[b]) for b in range(t0 + 2, len(w))}
        inverses = [None, None]
        for s in range(block):
            k, top, row = k0 + s, t0 + s // 8, s % 8
            inverse = 1.0 / jnp.broadcast_to(cols[top][s][row:row + 1], (8, n))
            old = inverses[s // 8]
            inverses[s // 8] = inverse if old is None else jnp.where(sub >= row, inverse, old)
            pivot_row = jnp.where(lane == k, 1.0, jnp.broadcast_to(w[top][row:row + 1], (8, n)))
            outside = jnp.where((lane > k) & (lane < k0 + block), 0.0, pivot_row)
            heads = [jnp.broadcast_to(cols[top][j][row:row + 1], (8, n)) for j in range(s + 1, block)]
            for b in close:
                if b < top or (b == top and row == 7):
                    continue
                f = cols[b][s] * inverse
                if b == top:
                    f = jnp.where(sub > row, f, 0.0)
                if b < t0 + 2:
                    at = (lane == k) & (sub > row) if b == top else lane == k
                    w[b] = jnp.where(at, 0.0, w[b]) - f * pivot_row
                else:
                    below[b] = below[b] - f * outside
                for j in range(s + 1, block):
                    cols[b][j] = cols[b][j] - f * heads[j - s - 1]
        if t0 + near < len(w):
            factors, rows = [], []
            for h in range(2):
                pivot = k0 + 8 * h + sub
                factors.append(w[t0 + h] * inverses[h])
                rows.append(jnp.where(lane == pivot, 1.0,
                                      jnp.where((lane > pivot) & (lane < k0 + block), 0.0, w[t0 + h])))
            update = lax.dot_general(jnp.concatenate(factors, axis=0), jnp.concatenate(rows, axis=0),
                                     (((0,), (0,)), ((), ())), precision=lax.Precision.HIGHEST,
                                     preferred_element_type=F32)
            for b in range(t0 + near, len(w)):
                below[b] = below[b] - update[8 * b:8 * b + 8]
        for b in below:
            w[b] = below[b]
    r, x = [], []
    for b in range(len(w)):
        diag = lane == sub + 8 * b
        scale = lax.rsqrt(jnp.sum(jnp.where(diag, w[b], 0.0), axis=1, keepdims=True))
        r.append(jnp.where(lane >= sub + 8 * b, w[b] * scale, 0.0))
        x.append(jnp.where(diag, scale, jnp.where(lane < sub + 8 * b, w[b] * scale, 0.0)))
    return jnp.concatenate(r, axis=0), jnp.concatenate(x, axis=0)


def modes_kernel(p_ref, an_ref, as_ref, ac_ref, a_ref, out_hbm, r_ref, x_ref, o_ref, sems, *, total):
    fields, cols, rows, width = out_hbm.shape
    quarter = cols // 4
    bounds = [quarter * q for q in range(5)]
    parts = [(f, lo, hi) for f in range(fields) for lo, hi in zip(bounds, bounds[1:])]
    parts[:1] = [(0, 0, quarter // 3), (0, quarter // 3, quarter)]
    g = unpack(p_ref[...]) * (1.0 / total)
    r, x = factor(tiles_of(g))
    r_ref[...] = r
    inv = x.T
    high = inv.astype(BF16)
    x_ref[0:width] = high
    x_ref[width:] = (inv - high.astype(F32)).astype(BF16)

    def times(a):
        return jnp.dot(jnp.concatenate([a, a], axis=1), x_ref[...], preferred_element_type=F32)

    def leave(i):
        f, lo, hi = parts[i]
        return pltpu.make_async_copy(o_ref.at[f, pl.ds(lo, hi - lo)], out_hbm.at[f, pl.ds(lo, hi - lo)], sems.at[i])

    for i, (f, lo, hi) in enumerate(parts):
        o_ref[f, lo:hi] = times(a_ref[f, lo:hi].reshape(-1, width)).reshape(hi - lo, rows, width)
        if lo == 0:
            north, south = times(an_ref[f]), times(as_ref[f])
        for l in range(lo, hi):
            if l < 2 or l >= cols - 2:
                o_ref[f, l] = times(ac_ref[f, l if l < 2 else l - cols + 4])
            else:
                o_ref[f, l, 0:2] = north[2 * l:2 * l + 2]
                o_ref[f, l, rows - 2:rows] = south[2 * l:2 * l + 2]
        leave(i).start()
    for i in range(len(parts)):
        leave(i).wait()


def exchanges(lon, lat):
    def device(k, z):
        return k * lat + z

    lon_a = [(k, k ^ 1) for k in range(lon)]
    lon_b = [(k, (k - 1 if k % 2 == 0 else k + 1) % lon) for k in range(lon)]
    lat_a = [(device(k, z), device(k, z ^ 1)) for k in range(lon) for z in range(lat)]
    lat_b = []
    for k in range(lon):
        for z in range(lat):
            to = z - 1 if z % 2 == 0 else z + 1
            lat_b.append((device(k, z), device(k, to) if 0 <= to < lat else device(k ^ 1, z)))
    return lon_a, lon_b, lat_a, lat_b


def halos(even, lon_a, lon_b, lat_a, lat_b):
    lon, lat = lax.axis_size("lon"), lax.axis_size("lat")
    by_lon_a, by_lon_b, by_lat_a, by_lat_b = exchanges(lon, lat)
    both = ("lon", "lat")
    fields, _, rows, width = lon_a.shape
    lat_b = lax.ppermute(lat_b, both, by_lat_b)
    lat_a = lax.ppermute(lat_a, both, by_lat_a)
    lon_b = lax.ppermute(lon_b, "lon", by_lon_b)
    lon_a = lax.ppermute(lon_a, "lon", by_lon_a)
    sides = jnp.concatenate([lon_a, lon_b], axis=1)
    low = sides[:, :, :2].reshape(fields, 8, width)
    high = sides[:, :, rows - 2:].reshape(fields, 8, width)
    even = jnp.broadcast_to(even[None] > 0.5, low.shape)
    corner_b = lax.ppermute(jnp.where(even, low, high), both, by_lat_b)
    corner_a = lax.ppermute(jnp.where(even, high, low), both, by_lat_a)
    return lon_a, lon_b, lat_a, lat_b, corner_a, corner_b


def total_gram(gram):
    lon, lat = lax.axis_size("lon"), lax.axis_size("lat")

    def partner(dk, dz):
        pairs = [(k * lat + z, (k ^ dk) * lat + (z ^ dz)) for k in range(lon) for z in range(lat)]
        return lax.ppermute(gram, ("lon", "lat"), pairs)

    gram = gram + partner(1, 0)
    by_lon = [1 << i for i in range(1, lon.bit_length() - 1)]
    by_lat = [1 << i for i in range(lat.bit_length() - 1)]
    while by_lon or by_lat:
        if by_lon and by_lat:
            dk, dz = by_lon.pop(0), by_lat.pop(0)
            x, z, xz = partner(dk ^ 1, 0), partner(1, dz), partner(dk ^ 1, dz)
            gram = (gram + x) + (z + xz)
        elif by_lon:
            gram = gram + partner(by_lon.pop(0) ^ 1, 0)
        else:
            gram = gram + partner(1, by_lat.pop(0))
    return gram


def local(members, background):
    fields, rows, cols, width = members.shape
    lat, lon = lax.axis_size("lat"), lax.axis_size("lon")
    nlat = rows * lat
    pairs = 2 * cols
    place = jnp.stack([lax.axis_index("lon"), lax.axis_index("lat")]).astype(jnp.int32)
    smem = pl.BlockSpec(memory_space=pltpu.SMEM)
    vmem = pl.BlockSpec(memory_space=pltpu.VMEM)
    hbm = pl.BlockSpec(memory_space=pl.ANY)
    params = pltpu.CompilerParams(vmem_limit_bytes=VMEM_LIMIT)

    def kept(*xs):
        return [pltpu.with_memory_space_constraint(x, pltpu.VMEM) for x in xs]

    m = pltpu.with_memory_space_constraint(jnp.transpose(members, (0, 2, 1, 3)), pltpu.HBM)
    m, near, even, *sent = pl.pallas_call(
        edges_kernel,
        out_shape=(pltpu.VMEM((fields, cols, rows, width), BF16), pltpu.VMEM((fields, 8, rows, width), BF16),
                   pltpu.VMEM(TILE, F32)) + (pltpu.VMEM((fields, 2, rows, width), BF16),) * 2
        + (pltpu.VMEM((fields, pairs, width), BF16),) * 2,
        in_specs=[smem, hbm],
        out_specs=(vmem,) * 7,
        scratch_shapes=[pltpu.VMEM((pairs, width), F32), pltpu.VMEM((pairs, width), F32),
                        pltpu.SemaphoreType.DMA((fields,))],
        compiler_params=params,
    )(place, m)
    beside = halos(even, *sent)
    a, en, es, gram = pl.pallas_call(
        functools.partial(inner_kernel, nlat=nlat),
        out_shape=(pltpu.VMEM((fields, cols, rows, width), BF16), pltpu.VMEM((fields, pairs, width), F32),
                   pltpu.VMEM((fields, pairs, width), F32), pltpu.VMEM((width, width), F32)),
        in_specs=[smem, vmem, vmem],
        out_specs=(vmem,) * 4,
        scratch_shapes=[pltpu.VMEM((256, 256), BF16), pltpu.VMEM((4, rows // 8, 8, 128), F32),
                        pltpu.VMEM((256, 256), F32)],
        compiler_params=params,
        cost_estimate=pl.CostEstimate(flops=16 * fields * cols * rows * width * width,
                                      bytes_accessed=8 * fields * cols * rows * width, transcendentals=0),
    )(place, *kept(m), background)
    an, as_, ac, packed = pl.pallas_call(
        functools.partial(outer_kernel, nlat=nlat),
        out_shape=(pltpu.VMEM((fields, pairs, width), BF16), pltpu.VMEM((fields, pairs, width), BF16),
                   pltpu.VMEM((fields, 4, rows, width), BF16), pltpu.VMEM((80, width), F32)),
        in_specs=[smem] + [vmem] * 11,
        out_specs=(vmem,) * 4,
        scratch_shapes=[pltpu.VMEM((2 * fields, pairs + 16, width), F32),
                        pltpu.VMEM((fields, 12, rows + 8, width), F32)],
        compiler_params=params,
    )(place, *kept(en, es, near, *beside, background, gram))
    packed = total_gram(packed)
    modes, r_factor = pl.pallas_call(
        functools.partial(modes_kernel, total=float(fields * nlat * cols * lon)),
        out_shape=(jax.ShapeDtypeStruct((fields, cols, rows, width), F32),
                   jax.ShapeDtypeStruct((width, width), F32)),
        in_specs=[vmem] * 5,
        out_specs=(hbm, vmem),
        scratch_shapes=[pltpu.VMEM((2 * width, width), BF16), pltpu.VMEM((fields, cols, rows, width), F32),
                        pltpu.SemaphoreType.DMA((fields * 4 + 1,))],
        compiler_params=params,
    )(*kept(packed, an, as_, ac, a))
    return jnp.transpose(modes, (0, 2, 1, 3)), r_factor


def solution(mesh):
    return jax.shard_map(
        local,
        mesh=mesh,
        in_specs=(P(None, "lat", "lon", None), P(None, "lat", "lon")),
        out_specs=(P(None, "lat", "lon", None), P()),
        check_vma=False,
    )
```

```python
import functools
import math

import jax
import jax.numpy as jnp
from jax import lax
from jax.experimental import pallas as pl
from jax.experimental.pallas import tpu as pltpu
from jax.sharding import PartitionSpec as P

VMEM_LIMIT = 32 * 1024 * 1024
F32 = jnp.float32
BF16 = jnp.bfloat16
TILE = (8, 128)


def row_coefs(glob, nlat):
    phi = (0.125 * (glob.astype(F32) + 0.5) - 0.0625 * nlat) * (math.pi / 180.0)
    square = phi * phi
    cosine = 0.0
    for power in range(14, -2, -2):
        cosine = cosine * square + (-1.0) ** (power // 2) / math.factorial(power)
    return 0.05 + 0.2 * (1.0 - cosine), jnp.sqrt(cosine)


def scaled_coefs(glob, nlat):
    kx, weight = row_coefs(glob, nlat)
    return 3.0 - 10.0 * kx, 5.0 * kx, weight


def sublane():
    return lax.broadcasted_iota(jnp.int32, TILE, 0)


def tiles_of(x):
    return [x[8 * t:8 * t + 8] for t in range(x.shape[0] // 8)]


def neighbours(x, above, below):
    sub = sublane()
    down = [pltpu.roll(t, 1, 0) for t in x]
    up = [pltpu.roll(t, 7, 0) for t in x]
    out = []
    for i in range(len(x)):
        north = jnp.where(sub == 0, down[i - 1] if i else above, down[i])
        south = jnp.where(sub == 7, up[i + 1] if i + 1 < len(x) else below, up[i])
        out.append(north + south)
    return out


def gram_of(a):
    return lax.dot_general(a, a, (((0,), (0,)), ((), ())), preferred_element_type=F32)


def tables(place_ref, mat_ref, coef_ref, edge_ref, entries_ref, rows, nlat):
    nt = rows // 8
    first = place_ref[1] * rows
    sub = sublane()
    lane = lax.broadcasted_iota(jnp.int32, TILE, 1)
    for t in range(nt):
        row = 8 * t + sub
        glob = first + row
        c, k, w = scaled_coefs(glob, nlat)
        cn, kn, _ = scaled_coefs(glob - 1, nlat)
        cs, ks, _ = scaled_coefs(glob + 1, nlat)
        live = (row >= 2) & (row < rows - 2)
        coef_ref[0, t], coef_ref[1, t] = 0.04 * w, w
        coef_ref[2, t], coef_ref[3, t] = jnp.where(live, 0.04 * w, 0.0), jnp.where(live, w, 0.0)
        both = jnp.where((glob == 0) | (glob == nlat - 1), 1.0, 2.0)
        dj = lax.rem(lane, rows) - row
        for i in range(4):
            for half in range(2):
                dl = jnp.abs(4 * half + lax.div(lane, rows) - i - 2)
                by_lon = lambda zero, one, two: jnp.where(
                    dl == 0, zero, jnp.where(dl == 1, one, jnp.where(dl == 2, two, 0.0)))
                entry = jnp.where(
                    dj == 0, by_lon(both + c * c + 2.0 * k * k, 2.0 * c * k, k * k), jnp.where(
                        dj == -1, by_lon(c + cn, k + kn, 0.0), jnp.where(
                            dj == 1, by_lon(c + cs, k + ks, 0.0), jnp.where(
                                (jnp.abs(dj) == 2) & (dl == 0), 1.0, 0.0))))
                high = entry.astype(BF16).astype(F32)
                at = pl.ds(rows * i + 8 * t, 8), pl.ds(128 * half, 128)
                entries_ref[at[0], at[1]] = high
                entries_ref[pl.ds(128 + rows * i + 8 * t, 8), at[1]] = entry - high
    mat_ref[...] = entries_ref[...].astype(BF16)

    def splat(row):
        return jnp.full(TILE, row, jnp.int32)

    for side, (near, halo, par, exists) in enumerate(((0, -1, 0, first > 0), (rows - 1, rows, 1, first + rows < nlat))):
        c0, k0, _ = scaled_coefs(splat(first + near), nlat)
        c1, k1, _ = scaled_coefs(splat(first + halo), nlat)
        _, _, w = scaled_coefs(splat(first + near) + (sub % 2 - par), nlat)
        outermost = sub % 2 == par
        edge_ref[side, 0] = jnp.where(outermost, c0 + c1, 0.0)
        edge_ref[side, 1] = jnp.where(outermost, k0 + k1, 0.0)
        edge_ref[side, 2] = jnp.where(exists, 0.04 * w, 0.0)
    for t in range(nt):
        edge_ref[2, t], edge_ref[3, t], edge_ref[4, t] = scaled_coefs(first + 8 * t + sub, nlat)
    beyond = first + rows + jnp.where(sub < 4, sub, sub - 8 - rows)
    real = (beyond >= 0) & (beyond < nlat)
    c, k, _ = scaled_coefs(beyond, nlat)
    edge_ref[2, nt], edge_ref[3, nt] = jnp.where(real, c, 0.0), jnp.where(real, k, 0.0)
    edge_ref[4, nt] = jnp.where(real, 1.0, 0.0)


def edges_kernel(place_ref, m_hbm, m_ref, near_ref, even_ref, mat_ref, coef_ref, edge_ref, lon_a_ref, lon_b_ref,
                 lat_a_ref, lat_b_ref, entries_ref, low_ref, high_ref, sems, *, nlat):
    fields, cols, rows, width = m_ref.shape
    lon_even = lax.rem(place_ref[0], 2) == 0
    lat_even = lax.rem(place_ref[1], 2) == 0
    even_ref[...] = jnp.where(jnp.full(even_ref.shape, lat_even, jnp.bool_), 1.0, 0.0)
    pieces = [(f, lo, hi) for f in range(fields) for lo, hi in ((0, cols // 16 * 8), (cols // 16 * 8, cols))]
    copies = [pltpu.make_async_copy(m_hbm.at[f, pl.ds(lo, hi - lo)], m_ref.at[f, pl.ds(lo, hi - lo)], sems.at[i])
              for i, (f, lo, hi) in enumerate(pieces)]
    for copy in copies:
        copy.start()
    tables(place_ref, mat_ref, coef_ref, edge_ref, entries_ref, rows, nlat)
    for copy, (f, lo, hi) in zip(copies, pieces):
        copy.wait()
        for l in range(lo, hi):
            low_ref[f, 2 * l:2 * l + 2] = m_ref[f, l, 0:16].astype(F32)[0:2]
            high_ref[f, 2 * l:2 * l + 2] = m_ref[f, l, rows - 16:rows].astype(F32)[14:16]
        low, high = low_ref[f, 2 * lo:2 * hi], high_ref[f, 2 * lo:2 * hi]
        lat_a_ref[f, 2 * lo:2 * hi] = jnp.where(lat_even, high, low).astype(BF16)
        lat_b_ref[f, 2 * lo:2 * hi] = jnp.where(lat_even, low, high).astype(BF16)
        if hi == cols:
            first, last = m_ref[f, 0:2], m_ref[f, cols - 2:cols]
            near_ref[f, 0:4] = m_ref[f, 0:4]
            near_ref[f, 4:8] = m_ref[f, cols - 4:cols]
            lon_a_ref[f] = jnp.where(lon_even, last, first)
            lon_b_ref[f] = jnp.where(lon_even, first, last)


def inner_kernel(m_ref, bg_ref, mat_ref, coef_ref, a_ref, en_ref, es_ref, g_ref):
    cols, rows = m_ref.shape[1], m_ref.shape[2]
    wide = 2
    nt = rows // 8
    @pl.loop(0, m_ref.shape[0])
    def _(f):
        ground = bg_ref[f].astype(F32)
        for l in (0, 1, cols - 2, cols - 1):
            a_ref[f, l] = jnp.zeros((rows, 128), BF16)
        for l0 in range(2, cols - 2, 4 * wide):
            chunk = [m_ref[f, l - 2:l + 6].reshape(256, 128) for l in range(l0, min(l0 + 4 * wide, cols - 2), 4)]
            y = jnp.dot(mat_ref[...], jnp.concatenate(chunk, axis=1), preferred_element_type=F32)
            y = y[:128] + y[128:]
            for q in range(len(chunk)):
                made = []
                for i in range(4):
                    l = l0 + 4 * q + i
                    for t in range(nt):
                        yt = y[rows * i + 8 * t:rows * i + 8 * t + 8, 128 * q:128 * q + 128]
                        b = jnp.broadcast_to(ground[8 * t:8 * t + 8, l:l + 1], TILE)
                        made.append(yt * coef_ref[2, t] - b * coef_ref[3, t])
                        if t == 0:
                            en_ref[f, 2 * l:2 * l + 2] = (yt * coef_ref[0, t] - b * coef_ref[1, t])[0:2]
                        if t == nt - 1:
                            es_ref[f, 2 * l:2 * l + 2] = (yt * coef_ref[0, t] - b * coef_ref[1, t])[6:8]
                made = jnp.concatenate(made, axis=0).astype(BF16)
                l = l0 + 4 * q
                a_ref[f, l:l + 4] = made.reshape(4, rows, 128)

    g_ref[...] = gram_of(a_ref[...].reshape(-1, 128))


def pack(g):
    lane = lax.broadcasted_iota(jnp.int32, (32, 128), 1)
    middle = jnp.where(lane < 32, pltpu.roll(g[96:128], 32, 1), g[32:64])
    last = jnp.where(lane[:16] < 64, pltpu.roll(g[80:96], 64, 1), g[64:80])
    return jnp.concatenate([g[0:32], middle, last], axis=0)


def unpack(p):
    upper = jnp.concatenate([p[0:80], pltpu.roll(p[64:80], 64, 1), pltpu.roll(p[32:64], 96, 1)], axis=0)
    row = lax.broadcasted_iota(jnp.int32, (128, 128), 0)
    col = lax.broadcasted_iota(jnp.int32, (128, 128), 1)
    return jnp.where(col >= row, upper, upper.T)


def outer_kernel(place_ref, en_ref, es_ref, near_ref, lon_a_ref, lon_b_ref, lat_a_ref, lat_b_ref, corner_a_ref,
                 corner_b_ref, bg_ref, gin_ref, table_ref, an_ref, as_ref, ac_ref, g_ref, pad_ref, x_ref, *, nlat):
    fields, pairs = lat_a_ref.shape[0], lat_a_ref.shape[1]
    rows, cols = bg_ref.shape[1], bg_ref.shape[2]
    first = place_ref[1] * rows
    lon_even = lax.rem(place_ref[0], 2) == 0
    lat_even = lax.rem(place_ref[1], 2) == 0
    has_north, has_south = first > 0, first + rows < nlat
    nt = rows // 8
    sub = sublane()
    gram = gin_ref[...]

    for e_ref, a_h_ref, b_h_ref, a_c_ref, b_c_ref, use_b, exists, out_ref, par, sign, at in (
            (en_ref, lat_a_ref, lat_b_ref, corner_a_ref, corner_b_ref, lat_even, has_north, an_ref, 0, 1, rows + 6),
            (es_ref, lat_b_ref, lat_a_ref, corner_b_ref, corner_a_ref, lat_even, has_south, as_ref, 1, -1, rows)):
        c, k, w = (jnp.concatenate([table_ref[par, i]] * (pairs // 8), axis=0) for i in range(3))
        for f in range(fields):
            h = jnp.where(use_b, b_h_ref[f], a_h_ref[f]).astype(F32)
            pad = pad_ref.at[fields * par + f]
            pad[8:8 + pairs] = h
            nearer = pad[8 + sign:8 + sign + pairs]
            wide = pad[8 + sign - 2:8 + sign - 2 + pairs] + pad[8 + sign + 2:8 + sign + 2 + pairs]
            made = e_ref[f] + w * (h + c * nearer + k * wide)
            made = jnp.concatenate([jnp.where(sub >= 4, made[:8], 0.0), made[8:pairs - 8],
                                    jnp.where(sub < 4, made[pairs - 8:], 0.0)], axis=0).astype(BF16)
            edge = jnp.where(exists, jnp.concatenate([h[:8], h[pairs - 8:]], axis=0), 0.0)
            out_ref[f] = made
            gram = gram + gram_of(made)
            for l in range(4):
                x_ref[f, 2 + l, at:at + 2] = edge[2 * l:2 * l + 2]
                x_ref[f, 6 + l, at:at + 2] = edge[8 + 2 * l:10 + 2 * l]
            corner = jnp.where(use_b, b_c_ref[f].astype(F32), a_c_ref[f].astype(F32))
            corner = jnp.where(exists, corner, 0.0)
            west = jnp.where(lon_even, corner[4:8], corner[0:4])
            east = jnp.where(lon_even, corner[0:4], corner[4:8])
            for l in range(2):
                x_ref[f, l, at:at + 2] = west[2 * l:2 * l + 2]
                x_ref[f, 10 + l, at:at + 2] = east[2 * l:2 * l + 2]
    for f in range(fields):
        for l in range(12):
            x_ref[f, l, rows + 2:rows + 6] = jnp.zeros((4, 128), F32)
        for l in range(4):
            x_ref[f, 2 + l, 0:rows] = near_ref[f, l].astype(F32)
            x_ref[f, 6 + l, 0:rows] = near_ref[f, 4 + l].astype(F32)
        for l in range(2):
            a, b = lon_a_ref[f, l].astype(F32), lon_b_ref[f, l].astype(F32)
            x_ref[f, l, 0:rows] = jnp.where(lon_even, b, a)
            x_ref[f, 10 + l, 0:rows] = jnp.where(lon_even, a, b)

    vc, vk = ([table_ref[2 + i, t] for t in range(nt + 1)] for i in range(2))
    one = table_ref[4, nt]
    for f in range(fields):
        bg = bg_ref[f].astype(F32)
        for side in range(2):
            u = [tiles_of(x_ref[f, 6 * side + l]) for l in range(6)]
            v = []
            for l in range(1, 5):
                ns = neighbours(u[l], pltpu.roll(u[l][nt], 1, 0), pltpu.roll(u[l][0], 7, 0))
                ns[nt] = one * ns[nt]
                v.append([ns[t] + vc[t] * u[l][t] + vk[t] * (u[l - 1][t] + u[l + 1][t]) for t in range(nt + 1)])
            for l in range(2):
                ns = neighbours(v[l + 1], pltpu.roll(v[l + 1][nt], 1, 0), pltpu.roll(v[l + 1][0], 7, 0))
                at = l + side * (cols - 2)
                parts = []
                for t in range(nt):
                    y = ns[t] + vc[t] * v[l + 1][t] + vk[t] * (v[l][t] + v[l + 2][t])
                    b = jnp.broadcast_to(bg[8 * t:8 * t + 8, at:at + 1], TILE)
                    parts.append((0.04 * y - b) * table_ref[4, t])
                ac_ref[f, 2 * side + l] = jnp.concatenate(parts, axis=0).astype(BF16)
    gram = gram + gram_of(ac_ref[...].reshape(-1, 128))
    g_ref[...] = pack(gram)


def factor(g):
    n, block, near = 128, 16, 4
    lane = lax.broadcasted_iota(jnp.int32, (8, n), 1)
    sub = sublane()
    w = list(g)
    for t0 in range(0, len(w), 2):
        k0 = 8 * t0
        close = range(t0, min(len(w), t0 + near))
        cols = {b: [jnp.broadcast_to(w[b][:, k0 + j:k0 + j + 1], (8, n)) for j in range(block)] for b in close}
        below = {b: jnp.where((lane >= k0) & (lane < k0 + block), 0.0, w[b]) for b in range(t0 + 2, len(w))}
        inverses = [None, None]
        for s in range(block):
            k, top, row = k0 + s, t0 + s // 8, s % 8
            inverse = 1.0 / jnp.broadcast_to(cols[top][s][row:row + 1], (8, n))
            old = inverses[s // 8]
            inverses[s // 8] = inverse if old is None else jnp.where(sub >= row, inverse, old)
            pivot_row = jnp.where(lane == k, 1.0, jnp.broadcast_to(w[top][row:row + 1], (8, n)))
            outside = jnp.where((lane > k) & (lane < k0 + block), 0.0, pivot_row)
            heads = [jnp.broadcast_to(cols[top][j][row:row + 1], (8, n)) for j in range(s + 1, block)]
            for b in close:
                if b < top or (b == top and row == 7):
                    continue
                f = cols[b][s] * inverse
                if b == top:
                    f = jnp.where(sub > row, f, 0.0)
                if b < t0 + 2:
                    at = (lane == k) & (sub > row) if b == top else lane == k
                    w[b] = jnp.where(at, 0.0, w[b]) - f * pivot_row
                else:
                    below[b] = below[b] - f * outside
                for j in range(s + 1, block):
                    cols[b][j] = cols[b][j] - f * heads[j - s - 1]
        if t0 + near < len(w):
            factors, rows = [], []
            for h in range(2):
                pivot = k0 + 8 * h + sub
                factors.append(w[t0 + h] * inverses[h])
                rows.append(jnp.where(lane == pivot, 1.0,
                                      jnp.where((lane > pivot) & (lane < k0 + block), 0.0, w[t0 + h])))
            update = lax.dot_general(jnp.concatenate(factors, axis=0), jnp.concatenate(rows, axis=0),
                                     (((0,), (0,)), ((), ())), precision=lax.Precision.HIGHEST,
                                     preferred_element_type=F32)
            for b in range(t0 + near, len(w)):
                below[b] = below[b] - update[8 * b:8 * b + 8]
        for b in below:
            w[b] = below[b]
    r, x = [], []
    for b in range(len(w)):
        diag = lane == sub + 8 * b
        scale = lax.rsqrt(jnp.sum(jnp.where(diag, w[b], 0.0), axis=1, keepdims=True))
        r.append(jnp.where(lane >= sub + 8 * b, w[b] * scale, 0.0))
        x.append(jnp.where(diag, scale, jnp.where(lane < sub + 8 * b, w[b] * scale, 0.0)))
    return jnp.concatenate(r, axis=0), jnp.concatenate(x, axis=0)


def modes_kernel(p_ref, an_ref, as_ref, ac_ref, a_ref, out_hbm, r_ref, x_ref, o_ref, sems, *, total):
    fields, cols, rows, width = out_hbm.shape
    quarter = cols // 4
    bounds = [quarter * q for q in range(5)]
    parts = [(f, lo, hi) for f in range(fields) for lo, hi in zip(bounds, bounds[1:])]
    parts[:1] = [(0, 0, quarter // 3), (0, quarter // 3, quarter)]
    g = unpack(p_ref[...]) * (1.0 / total)
    r, x = factor(tiles_of(g))
    r_ref[...] = r
    inv = x.T
    high = inv.astype(BF16)
    x_ref[0:width] = high
    x_ref[width:] = (inv - high.astype(F32)).astype(BF16)

    def times(a):
        return jnp.dot(jnp.concatenate([a, a], axis=1), x_ref[...], preferred_element_type=F32)

    def leave(i):
        f, lo, hi = parts[i]
        return pltpu.make_async_copy(o_ref.at[f, pl.ds(lo, hi - lo)], out_hbm.at[f, pl.ds(lo, hi - lo)], sems.at[i])

    for i, (f, lo, hi) in enumerate(parts):
        o_ref[f, lo:hi] = times(a_ref[f, lo:hi].reshape(-1, width)).reshape(hi - lo, rows, width)
        if lo == 0:
            north, south = times(an_ref[f]), times(as_ref[f])
        for l in range(lo, hi):
            if l < 2 or l >= cols - 2:
                o_ref[f, l] = times(ac_ref[f, l if l < 2 else l - cols + 4])
            else:
                o_ref[f, l, 0:2] = north[2 * l:2 * l + 2]
                o_ref[f, l, rows - 2:rows] = south[2 * l:2 * l + 2]
        leave(i).start()
    for i in range(len(parts)):
        leave(i).wait()


def exchanges(lon, lat):
    def device(k, z):
        return k * lat + z

    lon_a = [(k, k ^ 1) for k in range(lon)]
    lon_b = [(k, (k - 1 if k % 2 == 0 else k + 1) % lon) for k in range(lon)]
    lat_a = [(device(k, z), device(k, z ^ 1)) for k in range(lon) for z in range(lat)]
    lat_b = []
    for k in range(lon):
        for z in range(lat):
            to = z - 1 if z % 2 == 0 else z + 1
            lat_b.append((device(k, z), device(k, to) if 0 <= to < lat else device(k ^ 1, z)))
    return lon_a, lon_b, lat_a, lat_b


def halos(even, lon_a, lon_b, lat_a, lat_b):
    lon, lat = lax.axis_size("lon"), lax.axis_size("lat")
    by_lon_a, by_lon_b, by_lat_a, by_lat_b = exchanges(lon, lat)
    both = ("lon", "lat")
    fields, _, rows, width = lon_a.shape
    lat_b = lax.ppermute(lat_b, both, by_lat_b)
    lat_a = lax.ppermute(lat_a, both, by_lat_a)
    lon_b = lax.ppermute(lon_b, "lon", by_lon_b)
    lon_a = lax.ppermute(lon_a, "lon", by_lon_a)
    sides = jnp.concatenate([lon_a, lon_b], axis=1)
    low = sides[:, :, :2].reshape(fields, 8, width)
    high = sides[:, :, rows - 2:].reshape(fields, 8, width)
    even = jnp.broadcast_to(even[None] > 0.5, low.shape)
    corner_b = lax.ppermute(jnp.where(even, low, high), both, by_lat_b)
    corner_a = lax.ppermute(jnp.where(even, high, low), both, by_lat_a)
    return lon_a, lon_b, lat_a, lat_b, corner_a, corner_b


def total_gram(gram):
    lon, lat = lax.axis_size("lon"), lax.axis_size("lat")

    def partner(dk, dz):
        pairs = [(k * lat + z, (k ^ dk) * lat + (z ^ dz)) for k in range(lon) for z in range(lat)]
        return lax.ppermute(gram, ("lon", "lat"), pairs)

    gram = gram + partner(1, 0)
    by_lon = [1 << i for i in range(1, lon.bit_length() - 1)]
    by_lat = [1 << i for i in range(lat.bit_length() - 1)]
    while by_lon or by_lat:
        if by_lon and by_lat:
            dk, dz = by_lon.pop(0), by_lat.pop(0)
            x, z, xz = partner(dk ^ 1, 0), partner(1, dz), partner(dk ^ 1, dz)
            gram = (gram + x) + (z + xz)
        elif by_lon:
            gram = gram + partner(by_lon.pop(0) ^ 1, 0)
        else:
            gram = gram + partner(1, by_lat.pop(0))
    return gram


def local(members, background):
    fields, rows, cols, width = members.shape
    lat, lon = lax.axis_size("lat"), lax.axis_size("lon")
    nlat = rows * lat
    pairs = 2 * cols
    place = jnp.stack([lax.axis_index("lon"), lax.axis_index("lat")]).astype(jnp.int32)
    smem = pl.BlockSpec(memory_space=pltpu.SMEM)
    vmem = pl.BlockSpec(memory_space=pltpu.VMEM)
    hbm = pl.BlockSpec(memory_space=pl.ANY)
    params = pltpu.CompilerParams(vmem_limit_bytes=VMEM_LIMIT)

    def kept(*xs):
        return [pltpu.with_memory_space_constraint(x, pltpu.VMEM) for x in xs]

    m = pltpu.with_memory_space_constraint(jnp.transpose(members, (0, 2, 1, 3)), pltpu.HBM)
    m, near, even, mat, coef, table, *sent = pl.pallas_call(
        functools.partial(edges_kernel, nlat=nlat),
        out_shape=(pltpu.VMEM((fields, cols, rows, width), BF16), pltpu.VMEM((fields, 8, rows, width), BF16),
                   pltpu.VMEM(TILE, F32), pltpu.VMEM((256, 256), BF16), pltpu.VMEM((4, rows // 8, 8, 128), F32),
                   pltpu.VMEM((5, rows // 8 + 1, 8, 128), F32)) + (pltpu.VMEM((fields, 2, rows, width), BF16),) * 2
        + (pltpu.VMEM((fields, pairs, width), BF16),) * 2,
        in_specs=[smem, hbm],
        out_specs=(vmem,) * 10,
        scratch_shapes=[pltpu.VMEM((256, 256), F32), pltpu.VMEM((fields, pairs, width), F32),
                        pltpu.VMEM((fields, pairs, width), F32), pltpu.SemaphoreType.DMA((2 * fields,))],
        compiler_params=params,
    )(place, m)
    beside = halos(even, *sent)
    a, en, es, gram = pl.pallas_call(
        inner_kernel,
        out_shape=(pltpu.VMEM((fields, cols, rows, width), BF16), pltpu.VMEM((fields, pairs, width), F32),
                   pltpu.VMEM((fields, pairs, width), F32), pltpu.VMEM((width, width), F32)),
        in_specs=[vmem] * 4,
        out_specs=(vmem,) * 4,
        compiler_params=params,
        cost_estimate=pl.CostEstimate(flops=16 * fields * cols * rows * width * width,
                                      bytes_accessed=8 * fields * cols * rows * width, transcendentals=0),
    )(*kept(m), background, *kept(mat, coef))
    an, as_, ac, packed = pl.pallas_call(
        functools.partial(outer_kernel, nlat=nlat),
        out_shape=(pltpu.VMEM((fields, pairs, width), BF16), pltpu.VMEM((fields, pairs, width), BF16),
                   pltpu.VMEM((fields, 4, rows, width), BF16), pltpu.VMEM((80, width), F32)),
        in_specs=[smem] + [vmem] * 12,
        out_specs=(vmem,) * 4,
        scratch_shapes=[pltpu.VMEM((2 * fields, pairs + 16, width), F32),
                        pltpu.VMEM((fields, 12, rows + 8, width), F32)],
        compiler_params=params,
    )(place, *kept(en, es, near, *beside, background, gram, table))
    packed = total_gram(packed)
    modes, r_factor = pl.pallas_call(
        functools.partial(modes_kernel, total=float(fields * nlat * cols * lon)),
        out_shape=(jax.ShapeDtypeStruct((fields, cols, rows, width), F32),
                   jax.ShapeDtypeStruct((width, width), F32)),
        in_specs=[vmem] * 5,
        out_specs=(hbm, vmem),
        scratch_shapes=[pltpu.VMEM((2 * width, width), BF16), pltpu.VMEM((fields, cols, rows, width), F32),
                        pltpu.SemaphoreType.DMA((fields * 4 + 1,))],
        compiler_params=params,
    )(*kept(packed, an, as_, ac, a))
    return jnp.transpose(modes, (0, 2, 1, 3)), r_factor


def solution(mesh):
    return jax.shard_map(
        local,
        mesh=mesh,
        in_specs=(P(None, "lat", "lon", None), P(None, "lat", "lon")),
        out_specs=(P(None, "lat", "lon", None), P()),
        check_vma=False,
    )
```

```python
import functools
import math

import jax
import jax.numpy as jnp
from jax import lax
from jax.experimental import pallas as pl
from jax.experimental.pallas import tpu as pltpu
from jax.sharding import PartitionSpec as P

VMEM_LIMIT = 32 * 1024 * 1024
F32 = jnp.float32
BF16 = jnp.bfloat16
TILE = (8, 128)


def row_coefs(glob, nlat):
    phi = (0.125 * (glob.astype(F32) + 0.5) - 0.0625 * nlat) * (math.pi / 180.0)
    square = phi * phi
    cosine = 0.0
    for power in range(14, -2, -2):
        cosine = cosine * square + (-1.0) ** (power // 2) / math.factorial(power)
    return 0.05 + 0.2 * (1.0 - cosine), jnp.sqrt(cosine)


def scaled_coefs(glob, nlat):
    kx, weight = row_coefs(glob, nlat)
    return 3.0 - 10.0 * kx, 5.0 * kx, weight


def sublane():
    return lax.broadcasted_iota(jnp.int32, TILE, 0)


def tiles_of(x):
    return [x[8 * t:8 * t + 8] for t in range(x.shape[0] // 8)]


def neighbours(x, above, below):
    sub = sublane()
    down = [pltpu.roll(t, 1, 0) for t in x]
    up = [pltpu.roll(t, 7, 0) for t in x]
    out = []
    for i in range(len(x)):
        north = jnp.where(sub == 0, down[i - 1] if i else above, down[i])
        south = jnp.where(sub == 7, up[i + 1] if i + 1 < len(x) else below, up[i])
        out.append(north + south)
    return out


def gram_of(a):
    return lax.dot_general(a, a, (((0,), (0,)), ((), ())), preferred_element_type=F32)


def tables(place_ref, mat_ref, coef_ref, edge_ref, entries_ref, rows, nlat):
    nt = rows // 8
    first = place_ref[1] * rows
    sub = sublane()
    lane = lax.broadcasted_iota(jnp.int32, TILE, 1)
    for t in range(nt):
        row = 8 * t + sub
        glob = first + row
        c, k, w = scaled_coefs(glob, nlat)
        cn, kn, _ = scaled_coefs(glob - 1, nlat)
        cs, ks, _ = scaled_coefs(glob + 1, nlat)
        live = (row >= 2) & (row < rows - 2)
        coef_ref[0, t], coef_ref[1, t] = 0.04 * w, w
        coef_ref[2, t], coef_ref[3, t] = jnp.where(live, 0.04 * w, 0.0), jnp.where(live, w, 0.0)
        both = jnp.where((glob == 0) | (glob == nlat - 1), 1.0, 2.0)
        dj = lax.rem(lane, rows) - row
        for i in range(4):
            for half in range(2):
                dl = jnp.abs(4 * half + lax.div(lane, rows) - i - 2)
                by_lon = lambda zero, one, two: jnp.where(
                    dl == 0, zero, jnp.where(dl == 1, one, jnp.where(dl == 2, two, 0.0)))
                entry = jnp.where(
                    dj == 0, by_lon(both + c * c + 2.0 * k * k, 2.0 * c * k, k * k), jnp.where(
                        dj == -1, by_lon(c + cn, k + kn, 0.0), jnp.where(
                            dj == 1, by_lon(c + cs, k + ks, 0.0), jnp.where(
                                (jnp.abs(dj) == 2) & (dl == 0), 1.0, 0.0))))
                high = entry.astype(BF16).astype(F32)
                at = pl.ds(rows * i + 8 * t, 8), pl.ds(128 * half, 128)
                entries_ref[at[0], at[1]] = high
                entries_ref[pl.ds(128 + rows * i + 8 * t, 8), at[1]] = entry - high
    mat_ref[...] = entries_ref[...].astype(BF16)

    def splat(row):
        return jnp.full(TILE, row, jnp.int32)

    for side, (near, halo, par, exists) in enumerate(((0, -1, 0, first > 0), (rows - 1, rows, 1, first + rows < nlat))):
        c0, k0, _ = scaled_coefs(splat(first + near), nlat)
        c1, k1, _ = scaled_coefs(splat(first + halo), nlat)
        _, _, w = scaled_coefs(splat(first + near) + (sub % 2 - par), nlat)
        outermost = sub % 2 == par
        edge_ref[side, 0] = jnp.where(outermost, c0 + c1, 0.0)
        edge_ref[side, 1] = jnp.where(outermost, k0 + k1, 0.0)
        edge_ref[side, 2] = jnp.where(exists, 0.04 * w, 0.0)
    for t in range(nt):
        edge_ref[2, t], edge_ref[3, t], edge_ref[4, t] = scaled_coefs(first + 8 * t + sub, nlat)
    beyond = first + rows + jnp.where(sub < 4, sub, sub - 8 - rows)
    real = (beyond >= 0) & (beyond < nlat)
    c, k, _ = scaled_coefs(beyond, nlat)
    edge_ref[2, nt], edge_ref[3, nt] = jnp.where(real, c, 0.0), jnp.where(real, k, 0.0)
    edge_ref[4, nt] = jnp.where(real, 1.0, 0.0)


def edges_kernel(place_ref, m_hbm, m_ref, near_ref, even_ref, mat_ref, coef_ref, edge_ref, lon_a_ref, lon_b_ref,
                 lat_a_ref, lat_b_ref, entries_ref, low_ref, high_ref, sems, *, nlat):
    fields, cols, rows, width = m_ref.shape
    lon_even = lax.rem(place_ref[0], 2) == 0
    lat_even = lax.rem(place_ref[1], 2) == 0
    even_ref[...] = jnp.where(jnp.full(even_ref.shape, lat_even, jnp.bool_), 1.0, 0.0)
    pieces = [(f, lo, hi) for f in range(fields) for lo, hi in ((0, cols // 16 * 8), (cols // 16 * 8, cols))]
    copies = [pltpu.make_async_copy(m_hbm.at[f, pl.ds(lo, hi - lo)], m_ref.at[f, pl.ds(lo, hi - lo)], sems.at[i])
              for i, (f, lo, hi) in enumerate(pieces)]
    for copy in copies:
        copy.start()
    tables(place_ref, mat_ref, coef_ref, edge_ref, entries_ref, rows, nlat)
    for copy, (f, lo, hi) in zip(copies, pieces):
        copy.wait()
        for l in range(lo, hi):
            low_ref[f, 2 * l:2 * l + 2] = m_ref[f, l, 0:16].astype(F32)[0:2]
            high_ref[f, 2 * l:2 * l + 2] = m_ref[f, l, rows - 16:rows].astype(F32)[14:16]
        low, high = low_ref[f, 2 * lo:2 * hi], high_ref[f, 2 * lo:2 * hi]
        lat_a_ref[f, 2 * lo:2 * hi] = jnp.where(lat_even, high, low).astype(BF16)
        lat_b_ref[f, 2 * lo:2 * hi] = jnp.where(lat_even, low, high).astype(BF16)
        if hi == cols:
            first, last = m_ref[f, 0:2], m_ref[f, cols - 2:cols]
            near_ref[f, 0:4] = m_ref[f, 0:4]
            near_ref[f, 4:8] = m_ref[f, cols - 4:cols]
            lon_a_ref[f] = jnp.where(lon_even, last, first)
            lon_b_ref[f] = jnp.where(lon_even, first, last)


def inner_kernel(m_ref, bg_ref, mat_ref, coef_ref, a_ref, en_ref, es_ref, g_ref):
    cols, rows = m_ref.shape[1], m_ref.shape[2]
    wide = 2
    nt = rows // 8
    @pl.loop(0, m_ref.shape[0])
    def _(f):
        ground = bg_ref[f].astype(F32)
        for l in (0, 1, cols - 2, cols - 1):
            a_ref[f, l] = jnp.zeros((rows, 128), BF16)
        for l0 in range(2, cols - 2, 4 * wide):
            chunk = [m_ref[f, l - 2:l + 6].reshape(256, 128) for l in range(l0, min(l0 + 4 * wide, cols - 2), 4)]
            y = jnp.dot(mat_ref[...], jnp.concatenate(chunk, axis=1), preferred_element_type=F32)
            y = y[:128] + y[128:]
            for q in range(len(chunk)):
                made = []
                for i in range(4):
                    l = l0 + 4 * q + i
                    for t in range(nt):
                        yt = y[rows * i + 8 * t:rows * i + 8 * t + 8, 128 * q:128 * q + 128]
                        b = jnp.broadcast_to(ground[8 * t:8 * t + 8, l:l + 1], TILE)
                        made.append(yt * coef_ref[2, t] - b * coef_ref[3, t])
                        if t == 0:
                            en_ref[f, 2 * l:2 * l + 2] = (yt * coef_ref[0, t] - b * coef_ref[1, t])[0:2]
                        if t == nt - 1:
                            es_ref[f, 2 * l:2 * l + 2] = (yt * coef_ref[0, t] - b * coef_ref[1, t])[6:8]
                made = jnp.concatenate(made, axis=0).astype(BF16)
                l = l0 + 4 * q
                a_ref[f, l:l + 4] = made.reshape(4, rows, 128)

    g_ref[...] = gram_of(a_ref[...].reshape(-1, 128))


def pack(g):
    lane = lax.broadcasted_iota(jnp.int32, (32, 128), 1)
    middle = jnp.where(lane < 32, pltpu.roll(g[96:128], 32, 1), g[32:64])
    last = jnp.where(lane[:16] < 64, pltpu.roll(g[80:96], 64, 1), g[64:80])
    return jnp.concatenate([g[0:32], middle, last], axis=0)


def unpack(p):
    upper = jnp.concatenate([p[0:80], pltpu.roll(p[64:80], 64, 1), pltpu.roll(p[32:64], 96, 1)], axis=0)
    row = lax.broadcasted_iota(jnp.int32, (128, 128), 0)
    col = lax.broadcasted_iota(jnp.int32, (128, 128), 1)
    return jnp.where(col >= row, upper, upper.T)


def outer_kernel(place_ref, en_ref, es_ref, near_ref, lon_a_ref, lon_b_ref, lat_a_ref, lat_b_ref, corner_a_ref,
                 corner_b_ref, bg_ref, gin_ref, table_ref, an_ref, as_ref, ac_ref, g_ref, pad_ref, x_ref, *, nlat):
    fields, pairs = lat_a_ref.shape[0], lat_a_ref.shape[1]
    rows, cols = bg_ref.shape[1], bg_ref.shape[2]
    first = place_ref[1] * rows
    lon_even = lax.rem(place_ref[0], 2) == 0
    lat_even = lax.rem(place_ref[1], 2) == 0
    has_north, has_south = first > 0, first + rows < nlat
    nt = rows // 8
    sub = sublane()
    gram = gin_ref[...]

    for e_ref, a_h_ref, b_h_ref, a_c_ref, b_c_ref, use_b, exists, out_ref, par, sign, at in (
            (en_ref, lat_a_ref, lat_b_ref, corner_a_ref, corner_b_ref, lat_even, has_north, an_ref, 0, 1, rows + 6),
            (es_ref, lat_b_ref, lat_a_ref, corner_b_ref, corner_a_ref, lat_even, has_south, as_ref, 1, -1, rows)):
        c, k, w = (jnp.concatenate([table_ref[par, i]] * (pairs // 8), axis=0) for i in range(3))
        for f in range(fields):
            h = jnp.where(use_b, b_h_ref[f], a_h_ref[f]).astype(F32)
            pad = pad_ref.at[fields * par + f]
            pad[8:8 + pairs] = h
            nearer = pad[8 + sign:8 + sign + pairs]
            wide = pad[8 + sign - 2:8 + sign - 2 + pairs] + pad[8 + sign + 2:8 + sign + 2 + pairs]
            made = e_ref[f] + w * (h + c * nearer + k * wide)
            made = jnp.concatenate([jnp.where(sub >= 4, made[:8], 0.0), made[8:pairs - 8],
                                    jnp.where(sub < 4, made[pairs - 8:], 0.0)], axis=0).astype(BF16)
            edge = jnp.where(exists, jnp.concatenate([h[:8], h[pairs - 8:]], axis=0), 0.0)
            out_ref[f] = made
            gram = gram + gram_of(made)
            for l in range(4):
                x_ref[f, 2 + l, at:at + 2] = edge[2 * l:2 * l + 2]
                x_ref[f, 6 + l, at:at + 2] = edge[8 + 2 * l:10 + 2 * l]
            corner = jnp.where(use_b, b_c_ref[f].astype(F32), a_c_ref[f].astype(F32))
            corner = jnp.where(exists, corner, 0.0)
            west = jnp.where(lon_even, corner[4:8], corner[0:4])
            east = jnp.where(lon_even, corner[0:4], corner[4:8])
            for l in range(2):
                x_ref[f, l, at:at + 2] = west[2 * l:2 * l + 2]
                x_ref[f, 10 + l, at:at + 2] = east[2 * l:2 * l + 2]
    for f in range(fields):
        for l in range(12):
            x_ref[f, l, rows + 2:rows + 6] = jnp.zeros((4, 128), F32)
        for l in range(4):
            x_ref[f, 2 + l, 0:rows] = near_ref[f, l].astype(F32)
            x_ref[f, 6 + l, 0:rows] = near_ref[f, 4 + l].astype(F32)
        for l in range(2):
            a, b = lon_a_ref[f, l].astype(F32), lon_b_ref[f, l].astype(F32)
            x_ref[f, l, 0:rows] = jnp.where(lon_even, b, a)
            x_ref[f, 10 + l, 0:rows] = jnp.where(lon_even, a, b)

    vc, vk = ([table_ref[2 + i, t] for t in range(nt + 1)] for i in range(2))
    one = table_ref[4, nt]
    for f in range(fields):
        bg = bg_ref[f].astype(F32)
        for side in range(2):
            u = [tiles_of(x_ref[f, 6 * side + l]) for l in range(6)]
            v = []
            for l in range(1, 5):
                ns = neighbours(u[l], pltpu.roll(u[l][nt], 1, 0), pltpu.roll(u[l][0], 7, 0))
                ns[nt] = one * ns[nt]
                v.append([ns[t] + vc[t] * u[l][t] + vk[t] * (u[l - 1][t] + u[l + 1][t]) for t in range(nt + 1)])
            for l in range(2):
                ns = neighbours(v[l + 1], pltpu.roll(v[l + 1][nt], 1, 0), pltpu.roll(v[l + 1][0], 7, 0))
                at = l + side * (cols - 2)
                parts = []
                for t in range(nt):
                    y = ns[t] + vc[t] * v[l + 1][t] + vk[t] * (v[l][t] + v[l + 2][t])
                    b = jnp.broadcast_to(bg[8 * t:8 * t + 8, at:at + 1], TILE)
                    parts.append((0.04 * y - b) * table_ref[4, t])
                ac_ref[f, 2 * side + l] = jnp.concatenate(parts, axis=0).astype(BF16)
    gram = gram + gram_of(ac_ref[...].reshape(-1, 128))
    g_ref[...] = pack(gram)


def factor(g):
    n, block, near = 128, 16, 4
    lane = lax.broadcasted_iota(jnp.int32, (8, n), 1)
    sub = sublane()
    w = list(g)
    for t0 in range(0, len(w), 2):
        k0 = 8 * t0
        close = range(t0, min(len(w), t0 + near))
        cols = {b: [jnp.broadcast_to(w[b][:, k0 + j:k0 + j + 1], (8, n)) for j in range(block)] for b in close}
        below = {b: jnp.where((lane >= k0) & (lane < k0 + block), 0.0, w[b]) for b in range(t0 + 2, len(w))}
        inverses = [None, None]
        for s in range(0, block, 2):
            k, top, row = k0 + s, t0 + s // 8, s % 8
            p, q = (jnp.broadcast_to(cols[top][s + i][row:row + 1], (8, n)) for i in range(2))
            second = jnp.broadcast_to(cols[top][s + 1][row + 1:row + 2], (8, n))
            inverse, inverse2 = 1.0 / p, p / (p * second - q * q)
            ratio = q * inverse
            old = inverses[s // 8]
            both = jnp.where(sub > row, inverse2, inverse)
            inverses[s // 8] = both if old is None else jnp.where(sub >= row, both, old)
            pivot_row = jnp.where(lane == k, 1.0, jnp.broadcast_to(w[top][row:row + 1], (8, n)))
            next_row = jnp.where(lane == k, 0.0, jnp.broadcast_to(w[top][row + 1:row + 2], (8, n))) - ratio * pivot_row
            next_row = jnp.where(lane == k + 1, 1.0, next_row)
            outside = jnp.where((lane > k) & (lane < k0 + block), 0.0, pivot_row)
            outside2 = jnp.where((lane > k + 1) & (lane < k0 + block), 0.0, next_row)
            heads = [jnp.broadcast_to(cols[top][j][row:row + 1], (8, n)) for j in range(s + 2, block)]
            heads2 = [jnp.broadcast_to(cols[top][j][row + 1:row + 2], (8, n)) - ratio * heads[j - s - 2]
                      for j in range(s + 2, block)]
            for b in close:
                if b < top:
                    continue
                f = cols[b][s] * inverse
                f2 = (cols[b][s + 1] - f * q) * inverse2
                if b == top:
                    f, f2 = jnp.where(sub > row, f, 0.0), jnp.where(sub > row + 1, f2, 0.0)
                if b < t0 + 2:
                    here, here2 = lane == k, lane == k + 1
                    if b == top:
                        here, here2 = here & (sub > row), here2 & (sub > row + 1)
                    w[b] = jnp.where(here2, 0.0, jnp.where(here, 0.0, w[b]) - f * pivot_row) - f2 * next_row
                else:
                    below[b] = below[b] - (f * outside + f2 * outside2)
                for j in range(s + 2, block):
                    cols[b][j] = cols[b][j] - (f * heads[j - s - 2] + f2 * heads2[j - s - 2])
        if t0 + near < len(w):
            factors, rows = [], []
            for h in range(2):
                pivot = k0 + 8 * h + sub
                factors.append(w[t0 + h] * inverses[h])
                rows.append(jnp.where(lane == pivot, 1.0,
                                      jnp.where((lane > pivot) & (lane < k0 + block), 0.0, w[t0 + h])))
            update = lax.dot_general(jnp.concatenate(factors, axis=0), jnp.concatenate(rows, axis=0),
                                     (((0,), (0,)), ((), ())), precision=lax.Precision.HIGHEST,
                                     preferred_element_type=F32)
            for b in range(t0 + near, len(w)):
                below[b] = below[b] - update[8 * b:8 * b + 8]
        for b in below:
            w[b] = below[b]
    r, x = [], []
    for b in range(len(w)):
        diag = lane == sub + 8 * b
        scale = lax.rsqrt(jnp.sum(jnp.where(diag, w[b], 0.0), axis=1, keepdims=True))
        r.append(jnp.where(lane >= sub + 8 * b, w[b] * scale, 0.0))
        x.append(jnp.where(diag, scale, jnp.where(lane < sub + 8 * b, w[b] * scale, 0.0)))
    return jnp.concatenate(r, axis=0), jnp.concatenate(x, axis=0)


def modes_kernel(p_ref, an_ref, as_ref, ac_ref, a_ref, out_hbm, r_ref, x_ref, o_ref, sems, *, total):
    fields, cols, rows, width = out_hbm.shape
    quarter = cols // 4
    bounds = [quarter * q for q in range(5)]
    parts = [(f, lo, hi) for f in range(fields) for lo, hi in zip(bounds, bounds[1:])]
    parts[:1] = [(0, 0, quarter // 3), (0, quarter // 3, quarter)]
    g = unpack(p_ref[...]) * (1.0 / total)
    r, x = factor(tiles_of(g))
    r_ref[...] = r
    inv = x.T
    high = inv.astype(BF16)
    x_ref[0:width] = high
    x_ref[width:] = (inv - high.astype(F32)).astype(BF16)

    def times(a):
        return jnp.dot(jnp.concatenate([a, a], axis=1), x_ref[...], preferred_element_type=F32)

    def leave(i):
        f, lo, hi = parts[i]
        return pltpu.make_async_copy(o_ref.at[f, pl.ds(lo, hi - lo)], out_hbm.at[f, pl.ds(lo, hi - lo)], sems.at[i])

    for i, (f, lo, hi) in enumerate(parts):
        o_ref[f, lo:hi] = times(a_ref[f, lo:hi].reshape(-1, width)).reshape(hi - lo, rows, width)
        if i == 0:
            few = -(-2 * hi // 16) * 16
            north, south = times(an_ref[f, :few]), times(as_ref[f, :few])
        elif i == 1 or lo == 0:
            north, south = times(an_ref[f]), times(as_ref[f])
        for l in range(lo, hi):
            if l < 2 or l >= cols - 2:
                o_ref[f, l] = times(ac_ref[f, l if l < 2 else l - cols + 4])
            else:
                o_ref[f, l, 0:2] = north[2 * l:2 * l + 2]
                o_ref[f, l, rows - 2:rows] = south[2 * l:2 * l + 2]
        leave(i).start()
    for i in range(len(parts)):
        leave(i).wait()


def exchanges(lon, lat):
    def device(k, z):
        return k * lat + z

    lon_a = [(k, k ^ 1) for k in range(lon)]
    lon_b = [(k, (k - 1 if k % 2 == 0 else k + 1) % lon) for k in range(lon)]
    lat_a = [(device(k, z), device(k, z ^ 1)) for k in range(lon) for z in range(lat)]
    lat_b = []
    for k in range(lon):
        for z in range(lat):
            to = z - 1 if z % 2 == 0 else z + 1
            lat_b.append((device(k, z), device(k, to) if 0 <= to < lat else device(k ^ 1, z)))
    return lon_a, lon_b, lat_a, lat_b


def halos(even, lon_a, lon_b, lat_a, lat_b):
    lon, lat = lax.axis_size("lon"), lax.axis_size("lat")
    by_lon_a, by_lon_b, by_lat_a, by_lat_b = exchanges(lon, lat)
    both = ("lon", "lat")
    fields, _, rows, width = lon_a.shape
    lat_b = lax.ppermute(lat_b, both, by_lat_b)
    lat_a = lax.ppermute(lat_a, both, by_lat_a)
    lon_b = lax.ppermute(lon_b, "lon", by_lon_b)
    lon_a = lax.ppermute(lon_a, "lon", by_lon_a)
    sides = jnp.concatenate([lon_a, lon_b], axis=1)
    low = sides[:, :, :2].reshape(fields, 8, width)
    high = sides[:, :, rows - 2:].reshape(fields, 8, width)
    even = jnp.broadcast_to(even[None] > 0.5, low.shape)
    corner_b = lax.ppermute(jnp.where(even, low, high), both, by_lat_b)
    corner_a = lax.ppermute(jnp.where(even, high, low), both, by_lat_a)
    return lon_a, lon_b, lat_a, lat_b, corner_a, corner_b


def total_gram(gram):
    lon, lat = lax.axis_size("lon"), lax.axis_size("lat")

    def partner(dk, dz):
        pairs = [(k * lat + z, (k ^ dk) * lat + (z ^ dz)) for k in range(lon) for z in range(lat)]
        return lax.ppermute(gram, ("lon", "lat"), pairs)

    gram = gram + partner(1, 0)
    by_lon = [(1 << i, 0) for i in range(1, lon.bit_length() - 1)]
    by_lat = [(0, 1 << i) for i in range(lat.bit_length() - 1)]
    for steps in (by_lon, by_lat):
        while steps:
            dk, dz = steps.pop(0)
            if steps:
                ek, ez = steps.pop(0)
                e, d, de = partner(ek ^ 1, ez), partner(dk ^ 1, dz), partner(dk ^ ek ^ 1, dz ^ ez)
                gram = (gram + d) + (e + de)
            else:
                gram = gram + partner(dk ^ 1, dz)
    return gram


def local(members, background):
    fields, rows, cols, width = members.shape
    lat, lon = lax.axis_size("lat"), lax.axis_size("lon")
    nlat = rows * lat
    pairs = 2 * cols
    place = jnp.stack([lax.axis_index("lon"), lax.axis_index("lat")]).astype(jnp.int32)
    smem = pl.BlockSpec(memory_space=pltpu.SMEM)
    vmem = pl.BlockSpec(memory_space=pltpu.VMEM)
    hbm = pl.BlockSpec(memory_space=pl.ANY)
    params = pltpu.CompilerParams(vmem_limit_bytes=VMEM_LIMIT)

    def kept(*xs):
        return [pltpu.with_memory_space_constraint(x, pltpu.VMEM) for x in xs]

    m = pltpu.with_memory_space_constraint(jnp.transpose(members, (0, 2, 1, 3)), pltpu.HBM)
    m, near, even, mat, coef, table, *sent = pl.pallas_call(
        functools.partial(edges_kernel, nlat=nlat),
        out_shape=(pltpu.VMEM((fields, cols, rows, width), BF16), pltpu.VMEM((fields, 8, rows, width), BF16),
                   pltpu.VMEM(TILE, F32), pltpu.VMEM((256, 256), BF16), pltpu.VMEM((4, rows // 8, 8, 128), F32),
                   pltpu.VMEM((5, rows // 8 + 1, 8, 128), F32)) + (pltpu.VMEM((fields, 2, rows, width), BF16),) * 2
        + (pltpu.VMEM((fields, pairs, width), BF16),) * 2,
        in_specs=[smem, hbm],
        out_specs=(vmem,) * 10,
        scratch_shapes=[pltpu.VMEM((256, 256), F32), pltpu.VMEM((fields, pairs, width), F32),
                        pltpu.VMEM((fields, pairs, width), F32), pltpu.SemaphoreType.DMA((2 * fields,))],
        compiler_params=params,
    )(place, m)
    beside = halos(even, *sent)
    a, en, es, gram = pl.pallas_call(
        inner_kernel,
        out_shape=(pltpu.VMEM((fields, cols, rows, width), BF16), pltpu.VMEM((fields, pairs, width), F32),
                   pltpu.VMEM((fields, pairs, width), F32), pltpu.VMEM((width, width), F32)),
        in_specs=[vmem] * 4,
        out_specs=(vmem,) * 4,
        compiler_params=params,
        cost_estimate=pl.CostEstimate(flops=16 * fields * cols * rows * width * width,
                                      bytes_accessed=8 * fields * cols * rows * width, transcendentals=0),
    )(*kept(m), background, *kept(mat, coef))
    an, as_, ac, packed = pl.pallas_call(
        functools.partial(outer_kernel, nlat=nlat),
        out_shape=(pltpu.VMEM((fields, pairs, width), BF16), pltpu.VMEM((fields, pairs, width), BF16),
                   pltpu.VMEM((fields, 4, rows, width), BF16), pltpu.VMEM((80, width), F32)),
        in_specs=[smem] + [vmem] * 12,
        out_specs=(vmem,) * 4,
        scratch_shapes=[pltpu.VMEM((2 * fields, pairs + 16, width), F32),
                        pltpu.VMEM((fields, 12, rows + 8, width), F32)],
        compiler_params=params,
    )(place, *kept(en, es, near, *beside, background, gram, table))
    packed = total_gram(packed)
    modes, r_factor = pl.pallas_call(
        functools.partial(modes_kernel, total=float(fields * nlat * cols * lon)),
        out_shape=(jax.ShapeDtypeStruct((fields, cols, rows, width), F32),
                   jax.ShapeDtypeStruct((width, width), F32)),
        in_specs=[vmem] * 5,
        out_specs=(hbm, vmem),
        scratch_shapes=[pltpu.VMEM((2 * width, width), BF16), pltpu.VMEM((fields, cols, rows, width), F32),
                        pltpu.SemaphoreType.DMA((fields * 4 + 1,))],
        compiler_params=params,
    )(*kept(packed, an, as_, ac, a))
    return jnp.transpose(modes, (0, 2, 1, 3)), r_factor


def solution(mesh):
    return jax.shard_map(
        local,
        mesh=mesh,
        in_specs=(P(None, "lat", "lon", None), P(None, "lat", "lon")),
        out_specs=(P(None, "lat", "lon", None), P()),
        check_vma=False,
    )
```

```python
import functools
import math

import jax
import jax.numpy as jnp
from jax import lax
from jax.experimental import pallas as pl
from jax.experimental.pallas import tpu as pltpu
from jax.sharding import PartitionSpec as P

VMEM_LIMIT = 32 * 1024 * 1024
F32 = jnp.float32
BF16 = jnp.bfloat16
TILE = (8, 128)


def row_coefs(glob, nlat):
    phi = (0.125 * (glob.astype(F32) + 0.5) - 0.0625 * nlat) * (math.pi / 180.0)
    square = phi * phi
    cosine = 0.0
    for power in range(14, -2, -2):
        cosine = cosine * square + (-1.0) ** (power // 2) / math.factorial(power)
    return 0.05 + 0.2 * (1.0 - cosine), jnp.sqrt(cosine)


def scaled_coefs(glob, nlat):
    kx, weight = row_coefs(glob, nlat)
    return 3.0 - 10.0 * kx, 5.0 * kx, weight


def sublane():
    return lax.broadcasted_iota(jnp.int32, TILE, 0)


def tiles_of(x):
    return [x[8 * t:8 * t + 8] for t in range(x.shape[0] // 8)]


def neighbours(x, above, below):
    sub = sublane()
    down = [pltpu.roll(t, 1, 0) for t in x]
    up = [pltpu.roll(t, 7, 0) for t in x]
    out = []
    for i in range(len(x)):
        north = jnp.where(sub == 0, down[i - 1] if i else above, down[i])
        south = jnp.where(sub == 7, up[i + 1] if i + 1 < len(x) else below, up[i])
        out.append(north + south)
    return out


def gram_of(a):
    return lax.dot_general(a, a, (((0,), (0,)), ((), ())), preferred_element_type=F32)


def tables(place_ref, mat_ref, coef_ref, edge_ref, entries_ref, rows, nlat):
    nt = rows // 8
    first = place_ref[1] * rows
    sub = sublane()
    lane = lax.broadcasted_iota(jnp.int32, TILE, 1)
    for t in range(nt):
        row = 8 * t + sub
        glob = first + row
        c, k, w = scaled_coefs(glob, nlat)
        cn, kn, _ = scaled_coefs(glob - 1, nlat)
        cs, ks, _ = scaled_coefs(glob + 1, nlat)
        live = (row >= 2) & (row < rows - 2)
        coef_ref[0, t], coef_ref[1, t] = 0.04 * w, w
        coef_ref[2, t], coef_ref[3, t] = jnp.where(live, 0.04 * w, 0.0), jnp.where(live, w, 0.0)
        both = jnp.where((glob == 0) | (glob == nlat - 1), 1.0, 2.0)
        dj = lax.rem(lane, rows) - row
        for i in range(4):
            for half in range(2):
                dl = jnp.abs(4 * half + lax.div(lane, rows) - i - 2)
                by_lon = lambda zero, one, two: jnp.where(
                    dl == 0, zero, jnp.where(dl == 1, one, jnp.where(dl == 2, two, 0.0)))
                entry = jnp.where(
                    dj == 0, by_lon(both + c * c + 2.0 * k * k, 2.0 * c * k, k * k), jnp.where(
                        dj == -1, by_lon(c + cn, k + kn, 0.0), jnp.where(
                            dj == 1, by_lon(c + cs, k + ks, 0.0), jnp.where(
                                (jnp.abs(dj) == 2) & (dl == 0), 1.0, 0.0))))
                high = entry.astype(BF16).astype(F32)
                at = pl.ds(rows * i + 8 * t, 8), pl.ds(128 * half, 128)
                entries_ref[at[0], at[1]] = high
                entries_ref[pl.ds(128 + rows * i + 8 * t, 8), at[1]] = entry - high
    mat_ref[...] = entries_ref[...].astype(BF16)

    def splat(row):
        return jnp.full(TILE, row, jnp.int32)

    for side, (near, halo, par, exists) in enumerate(((0, -1, 0, first > 0), (rows - 1, rows, 1, first + rows < nlat))):
        c0, k0, _ = scaled_coefs(splat(first + near), nlat)
        c1, k1, _ = scaled_coefs(splat(first + halo), nlat)
        _, _, w = scaled_coefs(splat(first + near) + (sub % 2 - par), nlat)
        outermost = sub % 2 == par
        edge_ref[side, 0] = jnp.where(outermost, c0 + c1, 0.0)
        edge_ref[side, 1] = jnp.where(outermost, k0 + k1, 0.0)
        edge_ref[side, 2] = jnp.where(exists, 0.04 * w, 0.0)
    for t in range(nt):
        edge_ref[2, t], edge_ref[3, t], edge_ref[4, t] = scaled_coefs(first + 8 * t + sub, nlat)
    beyond = first + rows + jnp.where(sub < 4, sub, sub - 8 - rows)
    real = (beyond >= 0) & (beyond < nlat)
    c, k, _ = scaled_coefs(beyond, nlat)
    edge_ref[2, nt], edge_ref[3, nt] = jnp.where(real, c, 0.0), jnp.where(real, k, 0.0)
    edge_ref[4, nt] = jnp.where(real, 1.0, 0.0)


def edges_kernel(place_ref, m_hbm, m_ref, near_ref, even_ref, mat_ref, coef_ref, edge_ref, lon_a_ref, lon_b_ref,
                 lat_a_ref, lat_b_ref, entries_ref, low_ref, high_ref, sems, *, nlat):
    fields, cols, rows, width = m_ref.shape
    lon_even = lax.rem(place_ref[0], 2) == 0
    lat_even = lax.rem(place_ref[1], 2) == 0
    even_ref[...] = jnp.where(jnp.full(even_ref.shape, lat_even, jnp.bool_), 1.0, 0.0)
    pieces = [(f, lo, hi) for f in range(fields) for lo, hi in ((0, cols // 16 * 8), (cols // 16 * 8, cols))]
    copies = [pltpu.make_async_copy(m_hbm.at[f, pl.ds(lo, hi - lo)], m_ref.at[f, pl.ds(lo, hi - lo)], sems.at[i])
              for i, (f, lo, hi) in enumerate(pieces)]
    for copy in copies:
        copy.start()
    tables(place_ref, mat_ref, coef_ref, edge_ref, entries_ref, rows, nlat)
    for copy, (f, lo, hi) in zip(copies, pieces):
        copy.wait()
        for l in range(lo, hi):
            low_ref[f, 2 * l:2 * l + 2] = m_ref[f, l, 0:16].astype(F32)[0:2]
            high_ref[f, 2 * l:2 * l + 2] = m_ref[f, l, rows - 16:rows].astype(F32)[14:16]
        low, high = low_ref[f, 2 * lo:2 * hi], high_ref[f, 2 * lo:2 * hi]
        lat_a_ref[f, 2 * lo:2 * hi] = jnp.where(lat_even, high, low).astype(BF16)
        lat_b_ref[f, 2 * lo:2 * hi] = jnp.where(lat_even, low, high).astype(BF16)
        if hi == cols:
            first, last = m_ref[f, 0:2], m_ref[f, cols - 2:cols]
            near_ref[f, 0:4] = m_ref[f, 0:4]
            near_ref[f, 4:8] = m_ref[f, cols - 4:cols]
            lon_a_ref[f] = jnp.where(lon_even, last, first)
            lon_b_ref[f] = jnp.where(lon_even, first, last)


def inner_kernel(m_ref, bg_ref, mat_ref, coef_ref, a_ref, en_ref, es_ref, g_ref):
    cols, rows = m_ref.shape[1], m_ref.shape[2]
    wide = 2
    nt = rows // 8
    @pl.loop(0, m_ref.shape[0])
    def _(f):
        ground = bg_ref[f].astype(F32)
        for l in (0, 1, cols - 2, cols - 1):
            a_ref[f, l] = jnp.zeros((rows, 128), BF16)
        for l0 in range(2, cols - 2, 4 * wide):
            chunk = [m_ref[f, l - 2:l + 6].reshape(256, 128) for l in range(l0, min(l0 + 4 * wide, cols - 2), 4)]
            y = jnp.dot(mat_ref[...], jnp.concatenate(chunk, axis=1), preferred_element_type=F32)
            y = y[:128] + y[128:]
            for q in range(len(chunk)):
                made = []
                for i in range(4):
                    l = l0 + 4 * q + i
                    for t in range(nt):
                        yt = y[rows * i + 8 * t:rows * i + 8 * t + 8, 128 * q:128 * q + 128]
                        b = jnp.broadcast_to(ground[8 * t:8 * t + 8, l:l + 1], TILE)
                        made.append(yt * coef_ref[2, t] - b * coef_ref[3, t])
                        if t == 0:
                            en_ref[f, 2 * l:2 * l + 2] = (yt * coef_ref[0, t] - b * coef_ref[1, t])[0:2]
                        if t == nt - 1:
                            es_ref[f, 2 * l:2 * l + 2] = (yt * coef_ref[0, t] - b * coef_ref[1, t])[6:8]
                made = jnp.concatenate(made, axis=0).astype(BF16)
                l = l0 + 4 * q
                a_ref[f, l:l + 4] = made.reshape(4, rows, 128)

    g_ref[...] = gram_of(a_ref[...].reshape(-1, 128))


def pack(g):
    lane = lax.broadcasted_iota(jnp.int32, (32, 128), 1)
    middle = jnp.where(lane < 32, pltpu.roll(g[96:128], 32, 1), g[32:64])
    last = jnp.where(lane[:16] < 64, pltpu.roll(g[80:96], 64, 1), g[64:80])
    return jnp.concatenate([g[0:32], middle, last], axis=0)


def unpack(p):
    upper = jnp.concatenate([p[0:80], pltpu.roll(p[64:80], 64, 1), pltpu.roll(p[32:64], 96, 1)], axis=0)
    row = lax.broadcasted_iota(jnp.int32, (128, 128), 0)
    col = lax.broadcasted_iota(jnp.int32, (128, 128), 1)
    return jnp.where(col >= row, upper, upper.T)


def outer_kernel(place_ref, en_ref, es_ref, near_ref, lon_a_ref, lon_b_ref, lat_a_ref, lat_b_ref, corner_a_ref,
                 corner_b_ref, bg_ref, gin_ref, table_ref, an_ref, as_ref, ac_ref, g_ref, pad_ref, x_ref, *, nlat):
    fields, pairs = lat_a_ref.shape[0], lat_a_ref.shape[1]
    rows, cols = bg_ref.shape[1], bg_ref.shape[2]
    first = place_ref[1] * rows
    lon_even = lax.rem(place_ref[0], 2) == 0
    lat_even = lax.rem(place_ref[1], 2) == 0
    has_north, has_south = first > 0, first + rows < nlat
    nt = rows // 8
    sub = sublane()
    gram = gin_ref[...]

    for e_ref, a_h_ref, b_h_ref, a_c_ref, b_c_ref, use_b, exists, out_ref, par, sign, at in (
            (en_ref, lat_a_ref, lat_b_ref, corner_a_ref, corner_b_ref, lat_even, has_north, an_ref, 0, 1, rows + 6),
            (es_ref, lat_b_ref, lat_a_ref, corner_b_ref, corner_a_ref, lat_even, has_south, as_ref, 1, -1, rows)):
        c, k, w = (jnp.concatenate([table_ref[par, i]] * (pairs // 8), axis=0) for i in range(3))
        for f in range(fields):
            h = jnp.where(use_b, b_h_ref[f], a_h_ref[f]).astype(F32)
            pad = pad_ref.at[fields * par + f]
            pad[8:8 + pairs] = h
            nearer = pad[8 + sign:8 + sign + pairs]
            wide = pad[8 + sign - 2:8 + sign - 2 + pairs] + pad[8 + sign + 2:8 + sign + 2 + pairs]
            made = e_ref[f] + w * (h + c * nearer + k * wide)
            made = jnp.concatenate([jnp.where(sub >= 4, made[:8], 0.0), made[8:pairs - 8],
                                    jnp.where(sub < 4, made[pairs - 8:], 0.0)], axis=0).astype(BF16)
            edge = jnp.where(exists, jnp.concatenate([h[:8], h[pairs - 8:]], axis=0), 0.0)
            out_ref[f] = made
            gram = gram + gram_of(made)
            for l in range(4):
                x_ref[f, 2 + l, at:at + 2] = edge[2 * l:2 * l + 2]
                x_ref[f, 6 + l, at:at + 2] = edge[8 + 2 * l:10 + 2 * l]
            corner = jnp.where(use_b, b_c_ref[f].astype(F32), a_c_ref[f].astype(F32))
            corner = jnp.where(exists, corner, 0.0)
            west = jnp.where(lon_even, corner[4:8], corner[0:4])
            east = jnp.where(lon_even, corner[0:4], corner[4:8])
            for l in range(2):
                x_ref[f, l, at:at + 2] = west[2 * l:2 * l + 2]
                x_ref[f, 10 + l, at:at + 2] = east[2 * l:2 * l + 2]
    for f in range(fields):
        for l in range(12):
            x_ref[f, l, rows + 2:rows + 6] = jnp.zeros((4, 128), F32)
        for l in range(4):
            x_ref[f, 2 + l, 0:rows] = near_ref[f, l].astype(F32)
            x_ref[f, 6 + l, 0:rows] = near_ref[f, 4 + l].astype(F32)
        for l in range(2):
            a, b = lon_a_ref[f, l].astype(F32), lon_b_ref[f, l].astype(F32)
            x_ref[f, l, 0:rows] = jnp.where(lon_even, b, a)
            x_ref[f, 10 + l, 0:rows] = jnp.where(lon_even, a, b)

    vc, vk = ([table_ref[2 + i, t] for t in range(nt + 1)] for i in range(2))
    one = table_ref[4, nt]
    for f in range(fields):
        bg = bg_ref[f].astype(F32)
        for side in range(2):
            u = [tiles_of(x_ref[f, 6 * side + l]) for l in range(6)]
            v = []
            for l in range(1, 5):
                ns = neighbours(u[l], pltpu.roll(u[l][nt], 1, 0), pltpu.roll(u[l][0], 7, 0))
                ns[nt] = one * ns[nt]
                v.append([ns[t] + vc[t] * u[l][t] + vk[t] * (u[l - 1][t] + u[l + 1][t]) for t in range(nt + 1)])
            for l in range(2):
                ns = neighbours(v[l + 1], pltpu.roll(v[l + 1][nt], 1, 0), pltpu.roll(v[l + 1][0], 7, 0))
                at = l + side * (cols - 2)
                parts = []
                for t in range(nt):
                    y = ns[t] + vc[t] * v[l + 1][t] + vk[t] * (v[l][t] + v[l + 2][t])
                    b = jnp.broadcast_to(bg[8 * t:8 * t + 8, at:at + 1], TILE)
                    parts.append((0.04 * y - b) * table_ref[4, t])
                ac_ref[f, 2 * side + l] = jnp.concatenate(parts, axis=0).astype(BF16)
    gram = gram + gram_of(ac_ref[...].reshape(-1, 128))
    g_ref[...] = pack(gram)


def factor(g):
    n, block, near = 128, 16, 4
    lane = lax.broadcasted_iota(jnp.int32, (8, n), 1)
    sub = sublane()
    w = list(g)
    for t0 in range(0, len(w), 2):
        k0 = 8 * t0
        close = range(t0, min(len(w), t0 + near))
        cols = {b: [jnp.broadcast_to(w[b][:, k0 + j:k0 + j + 1], (8, n)) for j in range(block)] for b in close}
        below = {b: jnp.where((lane >= k0) & (lane < k0 + block), 0.0, w[b]) for b in range(t0 + 2, len(w))}
        inverses = [None, None]
        for s in range(block):
            k, top, row = k0 + s, t0 + s // 8, s % 8
            inverse = 1.0 / jnp.broadcast_to(cols[top][s][row:row + 1], (8, n))
            old = inverses[s // 8]
            inverses[s // 8] = inverse if old is None else jnp.where(sub >= row, inverse, old)
            pivot_row = jnp.where(lane == k, 1.0, jnp.broadcast_to(w[top][row:row + 1], (8, n)))
            outside = jnp.where((lane > k) & (lane < k0 + block), 0.0, pivot_row)
            heads = [jnp.broadcast_to(cols[top][j][row:row + 1], (8, n)) for j in range(s + 1, block)]
            for b in close:
                if b < top or (b == top and row == 7):
                    continue
                f = cols[b][s] * inverse
                if b == top:
                    f = jnp.where(sub > row, f, 0.0)
                if b < t0 + 2:
                    at = (lane == k) & (sub > row) if b == top else lane == k
                    w[b] = jnp.where(at, 0.0, w[b]) - f * pivot_row
                else:
                    below[b] = below[b] - f * outside
                for j in range(s + 1, block):
                    cols[b][j] = cols[b][j] - f * heads[j - s - 1]
        if t0 + near < len(w):
            factors, rows = [], []
            for h in range(2):
                pivot = k0 + 8 * h + sub
                factors.append(w[t0 + h] * inverses[h])
                rows.append(jnp.where(lane == pivot, 1.0,
                                      jnp.where((lane > pivot) & (lane < k0 + block), 0.0, w[t0 + h])))
            update = lax.dot_general(jnp.concatenate(factors, axis=0), jnp.concatenate(rows, axis=0),
                                     (((0,), (0,)), ((), ())), precision=lax.Precision.HIGHEST,
                                     preferred_element_type=F32)
            for b in range(t0 + near, len(w)):
                below[b] = below[b] - update[8 * b:8 * b + 8]
        for b in below:
            w[b] = below[b]
    r, x = [], []
    for b in range(len(w)):
        diag = lane == sub + 8 * b
        scale = lax.rsqrt(jnp.sum(jnp.where(diag, w[b], 0.0), axis=1, keepdims=True))
        r.append(jnp.where(lane >= sub + 8 * b, w[b] * scale, 0.0))
        x.append(jnp.where(diag, scale, jnp.where(lane < sub + 8 * b, w[b] * scale, 0.0)))
    return jnp.concatenate(r, axis=0), jnp.concatenate(x, axis=0)


def modes_kernel(p_ref, an_ref, as_ref, ac_ref, a_ref, out_hbm, r_ref, x_ref, o_ref, sems, *, total):
    fields, cols, rows, width = out_hbm.shape
    quarter = cols // 4
    bounds = [quarter * q for q in range(5)]
    parts = [(f, lo, hi) for f in range(fields) for lo, hi in zip(bounds, bounds[1:])]
    parts[:1] = [(0, 0, quarter // 3), (0, quarter // 3, quarter)]
    g = unpack(p_ref[...]) * (1.0 / total)
    r, x = factor(tiles_of(g))
    r_ref[...] = r
    inv = x.T
    high = inv.astype(BF16)
    x_ref[0:width] = high
    x_ref[width:] = (inv - high.astype(F32)).astype(BF16)

    def times(a):
        return jnp.dot(jnp.concatenate([a, a], axis=1), x_ref[...], preferred_element_type=F32)

    def leave(i):
        f, lo, hi = parts[i]
        return pltpu.make_async_copy(o_ref.at[f, pl.ds(lo, hi - lo)], out_hbm.at[f, pl.ds(lo, hi - lo)], sems.at[i])

    for i, (f, lo, hi) in enumerate(parts):
        o_ref[f, lo:hi] = times(a_ref[f, lo:hi].reshape(-1, width)).reshape(hi - lo, rows, width)
        if i == 0:
            few = -(-2 * hi // 16) * 16
            north, south = times(an_ref[f, :few]), times(as_ref[f, :few])
        elif i == 1 or lo == 0:
            north, south = times(an_ref[f]), times(as_ref[f])
        for l in range(lo, hi):
            if l < 2 or l >= cols - 2:
                o_ref[f, l] = times(ac_ref[f, l if l < 2 else l - cols + 4])
            else:
                o_ref[f, l, 0:2] = north[2 * l:2 * l + 2]
                o_ref[f, l, rows - 2:rows] = south[2 * l:2 * l + 2]
        leave(i).start()
    for i in range(len(parts)):
        leave(i).wait()


def exchanges(lon, lat):
    def device(k, z):
        return k * lat + z

    lon_a = [(k, k ^ 1) for k in range(lon)]
    lon_b = [(k, (k - 1 if k % 2 == 0 else k + 1) % lon) for k in range(lon)]
    lat_a = [(device(k, z), device(k, z ^ 1)) for k in range(lon) for z in range(lat)]
    lat_b = []
    for k in range(lon):
        for z in range(lat):
            to = z - 1 if z % 2 == 0 else z + 1
            lat_b.append((device(k, z), device(k, to) if 0 <= to < lat else device(k ^ 1, z)))
    return lon_a, lon_b, lat_a, lat_b


def halos(even, lon_a, lon_b, lat_a, lat_b):
    lon, lat = lax.axis_size("lon"), lax.axis_size("lat")
    by_lon_a, by_lon_b, by_lat_a, by_lat_b = exchanges(lon, lat)
    both = ("lon", "lat")
    fields, _, rows, width = lon_a.shape
    lat_b = lax.ppermute(lat_b, both, by_lat_b)
    lat_a = lax.ppermute(lat_a, both, by_lat_a)
    lon_b = lax.ppermute(lon_b, "lon", by_lon_b)
    lon_a = lax.ppermute(lon_a, "lon", by_lon_a)
    sides = jnp.concatenate([lon_a, lon_b], axis=1)
    low = sides[:, :, :2].reshape(fields, 8, width)
    high = sides[:, :, rows - 2:].reshape(fields, 8, width)
    even = jnp.broadcast_to(even[None] > 0.5, low.shape)
    corner_b = lax.ppermute(jnp.where(even, low, high), both, by_lat_b)
    corner_a = lax.ppermute(jnp.where(even, high, low), both, by_lat_a)
    return lon_a, lon_b, lat_a, lat_b, corner_a, corner_b


def total_gram(gram):
    lon, lat = lax.axis_size("lon"), lax.axis_size("lat")

    def partner(dk, dz):
        pairs = [(k * lat + z, (k ^ dk) * lat + (z ^ dz)) for k in range(lon) for z in range(lat)]
        return lax.ppermute(gram, ("lon", "lat"), pairs)

    gram = gram + partner(1, 0)
    by_lon = [(1 << i, 0) for i in range(1, lon.bit_length() - 1)]
    by_lat = [(0, 1 << i) for i in range(lat.bit_length() - 1)]
    for steps in (by_lon, by_lat):
        while steps:
            dk, dz = steps.pop(0)
            if steps:
                ek, ez = steps.pop(0)
                e, d, de = partner(ek ^ 1, ez), partner(dk ^ 1, dz), partner(dk ^ ek ^ 1, dz ^ ez)
                gram = (gram + d) + (e + de)
            else:
                gram = gram + partner(dk ^ 1, dz)
    return gram


def local(members, background):
    fields, rows, cols, width = members.shape
    lat, lon = lax.axis_size("lat"), lax.axis_size("lon")
    nlat = rows * lat
    pairs = 2 * cols
    place = jnp.stack([lax.axis_index("lon"), lax.axis_index("lat")]).astype(jnp.int32)
    smem = pl.BlockSpec(memory_space=pltpu.SMEM)
    vmem = pl.BlockSpec(memory_space=pltpu.VMEM)
    hbm = pl.BlockSpec(memory_space=pl.ANY)
    params = pltpu.CompilerParams(vmem_limit_bytes=VMEM_LIMIT)

    def kept(*xs):
        return [pltpu.with_memory_space_constraint(x, pltpu.VMEM) for x in xs]

    m = pltpu.with_memory_space_constraint(jnp.transpose(members, (0, 2, 1, 3)), pltpu.HBM)
    m, near, even, mat, coef, table, *sent = pl.pallas_call(
        functools.partial(edges_kernel, nlat=nlat),
        out_shape=(pltpu.VMEM((fields, cols, rows, width), BF16), pltpu.VMEM((fields, 8, rows, width), BF16),
                   pltpu.VMEM(TILE, F32), pltpu.VMEM((256, 256), BF16), pltpu.VMEM((4, rows // 8, 8, 128), F32),
                   pltpu.VMEM((5, rows // 8 + 1, 8, 128), F32)) + (pltpu.VMEM((fields, 2, rows, width), BF16),) * 2
        + (pltpu.VMEM((fields, pairs, width), BF16),) * 2,
        in_specs=[smem, hbm],
        out_specs=(vmem,) * 10,
        scratch_shapes=[pltpu.VMEM((256, 256), F32), pltpu.VMEM((fields, pairs, width), F32),
                        pltpu.VMEM((fields, pairs, width), F32), pltpu.SemaphoreType.DMA((2 * fields,))],
        compiler_params=params,
    )(place, m)
    beside = halos(even, *sent)
    a, en, es, gram = pl.pallas_call(
        inner_kernel,
        out_shape=(pltpu.VMEM((fields, cols, rows, width), BF16), pltpu.VMEM((fields, pairs, width), F32),
                   pltpu.VMEM((fields, pairs, width), F32), pltpu.VMEM((width, width), F32)),
        in_specs=[vmem] * 4,
        out_specs=(vmem,) * 4,
        compiler_params=params,
        cost_estimate=pl.CostEstimate(flops=16 * fields * cols * rows * width * width,
                                      bytes_accessed=8 * fields * cols * rows * width, transcendentals=0),
    )(*kept(m), background, *kept(mat, coef))
    an, as_, ac, packed = pl.pallas_call(
        functools.partial(outer_kernel, nlat=nlat),
        out_shape=(pltpu.VMEM((fields, pairs, width), BF16), pltpu.VMEM((fields, pairs, width), BF16),
                   pltpu.VMEM((fields, 4, rows, width), BF16), pltpu.VMEM((80, width), F32)),
        in_specs=[smem] + [vmem] * 12,
        out_specs=(vmem,) * 4,
        scratch_shapes=[pltpu.VMEM((2 * fields, pairs + 16, width), F32),
                        pltpu.VMEM((fields, 12, rows + 8, width), F32)],
        compiler_params=params,
    )(place, *kept(en, es, near, *beside, background, gram, table))
    packed = total_gram(packed)
    modes, r_factor = pl.pallas_call(
        functools.partial(modes_kernel, total=float(fields * nlat * cols * lon)),
        out_shape=(jax.ShapeDtypeStruct((fields, cols, rows, width), F32),
                   jax.ShapeDtypeStruct((width, width), F32)),
        in_specs=[vmem] * 5,
        out_specs=(hbm, vmem),
        scratch_shapes=[pltpu.VMEM((2 * width, width), BF16), pltpu.VMEM((fields, cols, rows, width), F32),
                        pltpu.SemaphoreType.DMA((fields * 4 + 1,))],
        compiler_params=params,
    )(*kept(packed, an, as_, ac, a))
    return jnp.transpose(modes, (0, 2, 1, 3)), r_factor


def solution(mesh):
    return jax.shard_map(
        local,
        mesh=mesh,
        in_specs=(P(None, "lat", "lon", None), P(None, "lat", "lon")),
        out_specs=(P(None, "lat", "lon", None), P()),
        check_vma=False,
    )
```
